128 devices in a mesh: expert: 16 (over z_hi, y, core), dp: 8 (over x, z_lo).
Axes of the slice: x: 4, y: 4, z: 4 (z_hi: 2, z_lo: 2; z = z_hi * 2 + z_lo), core: 2. Of those that a mesh axis runs over, the one named last changes fastest.
Arguments:
- tokens: bfloat16 [16384, 2048], P(('expert', 'dp')), may hold values from -6 to 6
- cotangent: bfloat16 [16384, 2048], P(('expert', 'dp')), may hold values from -6 to 6
- gate_prob: float32 [16384], P(('expert', 'dp')), may hold values from 0.2 to 1
- expert_of: int32 [16384, 1], P(('expert', 'dp')), may hold values from 0 to 31; in each aligned block of 128 rows (0 to 127, 128 to 255, ...) at most 6 rows name the same one
- w_in: bfloat16 [32, 2048, 5120], P('expert', None, 'dp'), may hold values from -0.125 to 0.125
- w_out: bfloat16 [32, 5120, 2048], P('expert', 'dp'), may hold values from -0.078125 to 0.078125
Outputs:
- layer_out: bfloat16 [16384, 2048], P(('expert', 'dp'))
- grad_in: bfloat16 [32, 2048, 5120], P('expert', None, 'dp')
- grad_out: bfloat16 [32, 5120, 2048], P('expert', 'dp')
The draws below stay inside these ranges and needn't reach their ends.
Inputs may be any that keep to these rules, and one draw needn't show every extreme that they name: `expert_of`: among one device's 128 tokens no expert is named more than 6 times, and in every draw some device names some expert exactly 6 times.
All inputs are finite; a program needn't handle non-finite values.
Results may differ from the reference program's by a relative error of at most 0.015.
Values may be sent and summed in bfloat16 or wider, within the bound.
A program may use at most 128 MiB of HBM per device.

```python
import math
import jax
import jax.numpy as jnp
import numpy as np
from jax import lax

D = 2048
FF = 5120
TOK_DEV = 128
TILE_ROWS = 128
EXPERTS = 32
FF_DEV = 640
TOKENS = 16384
CAPE = 6
N_DP = 8


def steps_of(own_key, dims, split, least, top_value):
    loudness = 1.0
    for axis_at, parts in split:
        heights = jax.random.uniform(jax.random.fold_in(jax.random.fold_in(own_key, 6), axis_at), (parts,), jnp.float32, least / len(split), top_value / len(split))
        loudness = loudness * jnp.repeat(jnp.exp(heights), dims[axis_at] // parts).reshape((-1,) + (1,) * (len(dims) - 1 - axis_at))
    return loudness


def assign_block(rng, own, number, rows, amount, top, most, lean):
    order = jax.random.permutation(rng, amount)
    crowded, common = shares(amount, rows * top, most, lean, True), shares(amount, rows * top, most, lean, False)
    places = jnp.arange(amount)

    def named(tallies, turn):
        used = int((tallies > 0).sum())
        fixed = max(1, used // 4)
        moved = fixed + (places - fixed + turn * (used - fixed)) % max(1, amount - fixed)
        return jnp.zeros((amount,), jnp.int32).at[order[jnp.where(places < fixed, places, moved)]].set(jnp.asarray(tallies, jnp.int32))

    tallies = jnp.where(number % 4 == 0, named(crowded, number // 4), named(common, number - number // 4 - 1))
    mixed = jax.random.permutation(jax.random.fold_in(own, 3), amount)
    source_of, receiver = mixed[0:amount // 2 * 2:2], mixed[1:amount // 2 * 2:2]
    slack = jnp.minimum(tallies[source_of] - 1, most - tallies[receiver]) // 2
    slack = jnp.where((source_of == order[0]) | (receiver == order[0]) | (tallies[receiver] == 0), 0, jnp.maximum(slack, 0))
    moved = jax.random.randint(jax.random.fold_in(own, 4), (amount // 2,), 0, 1 << 20) % (slack + 1)
    tallies = tallies.at[source_of].add(-moved).at[receiver].add(moved)
    members = jnp.searchsorted(jnp.cumsum(tallies), jnp.arange(rows * top), side="right").astype(jnp.int32)
    grid = members.reshape(top, rows).T
    grid = grid[jax.random.permutation(jax.random.fold_in(own, 1), rows)]
    turn = jax.random.randint(jax.random.fold_in(own, 2), (rows, 1), 0, top)
    return jnp.take_along_axis(grid, (jnp.arange(top)[None, :] + turn) % top, axis=1)


def shares(amount, total, limit, skew, full):
    loads = [(1 << 20) // math.isqrt(rank ** skew) + 1 for rank in range(1, amount + 1)]
    largest = limit if full else min(limit, max(-(-total // amount), total * loads[0] // sum(loads)))
    least = 1 if total - largest >= amount - 1 else 0
    holding, spare = [largest] + [least] * (amount - 1), total - largest - least * (amount - 1)
    while spare > 0:
        free = [i for i in range(1, amount) if holding[i] < largest] or [i for i in range(1, amount) if holding[i] < limit]
        whole, left = sum([loads[i] for i in free]), spare
        for i in free:
            addition = min(limit - holding[i], max(1, left * loads[i] // whole), spare)
            holding[i] = holding[i] + addition
            spare = spare - addition
    return np.array(holding)


def normal_values(key, extent, deviation, reach, cuts=(), held_as=jnp.bfloat16):
    entries = jax.random.normal(key, extent, jnp.float32) * deviation
    if len(cuts) > 0:
        entries = steps_of(key, extent, cuts, -0.22, 0.18) * entries
    return jnp.clip(entries, min=-reach, max=reach).astype(held_as)


def setup_inputs(seed: int = 0) -> dict:
    keys = jax.random.split(jax.random.key(seed), 7)
    tokens = normal_values(keys[0], (TOKENS, D), 1.0, 6.0, ((0, 128),))
    cotangent = normal_values(keys[1], (TOKENS, D), 1.0, 6.0, ((0, 128),))
    gate_prob = jnp.clip(0.2 + 0.8 * jax.random.uniform(keys[2], (TOKENS,), jnp.float32) ** steps_of(keys[2], (TOKENS,), ((0, 128),), -0.2, 0.2), 0.2, 1.0)
    expert_of_keys = jax.random.split(jax.random.fold_in(keys[3], 1), TOKENS // TOK_DEV)
    expert_of_turns = jax.random.permutation(jax.random.fold_in(keys[3], 3), TOKENS // TOK_DEV)
    expert_of = jax.vmap(lambda own, number: assign_block(jax.random.fold_in(keys[3], 2), own, number, TOK_DEV, EXPERTS, 1, CAPE, 2))(expert_of_keys, expert_of_turns).reshape((TOKENS, 1))
    w_in = normal_values(keys[4], (EXPERTS, D, FF), D ** -0.5, 0.125, ((0, 16), (2, 8)))
    w_out = normal_values(keys[5], (EXPERTS, FF, D), FF ** -0.5, 0.078125, ((0, 16), (1, 8)))
    return dict(tokens=tokens, cotangent=cotangent, gate_prob=gate_prob, expert_of=expert_of, w_in=w_in, w_out=w_out)


ROOT = 0.7978845608028654
CUBIC = 0.044715


def gelu_pair(pre_act):
    tanh_arg = ROOT * (pre_act + CUBIC * pre_act * pre_act * pre_act)
    tangent = jnp.tanh(tanh_arg)
    gelu_value = 0.5 * pre_act * (1.0 + tangent)
    gelu_slope = 0.5 * (1.0 + tangent) + 0.5 * pre_act * (1.0 - tangent * tangent) * ROOT * (1.0 + 3.0 * CUBIC * pre_act * pre_act)
    return gelu_value, gelu_slope


def reference(tokens, cotangent, gate_prob, expert_of, w_in, w_out):
    labels = expert_of[:, 0].astype(jnp.int32)
    catalog = jnp.arange(EXPERTS, dtype=jnp.int32)
    counts = jnp.sum((labels[:, None] == catalog[None, :]).astype(jnp.int32), axis=0).astype(jnp.int32)
    starts = (jnp.cumsum(counts) - counts).astype(jnp.int32)
    padded = ((counts + TILE_ROWS - 1) // TILE_ROWS) * TILE_ROWS
    pad_starts = (jnp.cumsum(padded) - padded).astype(jnp.int32)
    ordering = jnp.argsort(labels, stable=True).astype(jnp.int32)
    scaled = (gate_prob[:, None] * cotangent.astype(jnp.float32)).astype(jnp.bfloat16)
    blocks = (TOKENS + TILE_ROWS - 1) // TILE_ROWS + EXPERTS
    offsets = jnp.arange(TILE_ROWS, dtype=jnp.int32)

    def one_block(totals, block_index):
        acc_in, acc_out = totals
        first_row = block_index * TILE_ROWS
        expert = jnp.clip(jnp.sum((pad_starts <= first_row).astype(jnp.int32)) - 1, 0, EXPERTS - 1).astype(jnp.int32)
        within = (first_row - pad_starts[expert] + offsets).astype(jnp.int32)
        inside = within < counts[expert]
        picked = ordering[jnp.clip(starts[expert] + within, 0, TOKENS - 1).astype(jnp.int32)]
        picked_rows = jnp.where(inside[:, None], tokens[picked], jnp.zeros((), jnp.bfloat16))
        cotangent_rows = jnp.where(inside[:, None], scaled[picked], jnp.zeros((), jnp.bfloat16))
        w_first = w_in[expert]
        w_second = w_out[expert]
        pre_act = jnp.dot(picked_rows, w_first, preferred_element_type=jnp.float32)
        gelu_value, gelu_slope = gelu_pair(pre_act)
        hidden = gelu_value.astype(jnp.bfloat16)
        pieces = jnp.einsum("bgf,gfd->gbd", hidden.reshape(TILE_ROWS, N_DP, FF_DEV).astype(jnp.float32), w_second.reshape(N_DP, FF_DEV, D).astype(jnp.float32))
        rounded = lax.optimization_barrier(pieces.astype(jnp.bfloat16))
        expert_sum = jnp.sum(rounded.astype(jnp.float32), axis=0)
        back_hidden = (jnp.dot(cotangent_rows, w_second.T, preferred_element_type=jnp.float32) * gelu_slope).astype(jnp.bfloat16)
        acc_out = acc_out.at[expert].add(jnp.dot(hidden.T, cotangent_rows, preferred_element_type=jnp.float32))
        acc_in = acc_in.at[expert].add(jnp.dot(picked_rows.T, back_hidden, preferred_element_type=jnp.float32))
        target = jnp.where(inside, picked, TOKENS).astype(jnp.int32)
        return (acc_in, acc_out), (expert_sum, target)

    initial = (jnp.zeros((EXPERTS, D, FF), jnp.float32), jnp.zeros((EXPERTS, FF, D), jnp.float32))
    (acc_in, acc_out), (expert_sums, targets) = lax.scan(one_block, initial, jnp.arange(blocks, dtype=jnp.int32))
    gathered = jnp.zeros((TOKENS, D), jnp.float32).at[targets.reshape(-1)].set(expert_sums.reshape(-1, D), mode="drop")
    layer_out = (gate_prob[:, None] * gathered).astype(jnp.bfloat16)
    return layer_out, acc_in.astype(jnp.bfloat16), acc_out.astype(jnp.bfloat16)
```

```python
import functools

import jax
import jax.numpy as jnp
import numpy as np
from jax import lax
from jax.experimental import pallas as pl
from jax.experimental.pallas import tpu as pltpu
from jax.sharding import PartitionSpec as P

ROOT = 0.7978845608028654
CUBIC = 0.044715
BF = jnp.bfloat16
F32 = jnp.float32
MESH = pl.DeviceIdType.MESH
CAP = 6
LOCAL = 2
SLOT = 16
NG = 16
NX = 4
ND = 8
HALF = NG * CAP
ROWS = LOCAL * HALF

AG = ("z1", "z20", "z2m", "z2p", "z22", "xp1", "xm1", "xp2", "xm2", "xp1z", "xm1z",
      "fp1", "fm1", "fp2", "fm2", "fp1z", "fm1z")
RS = ("a0", "a1", "b0", "b1", "c0", "c1", "d0", "d1", "z", "q0", "q1", "q2", "q3",
      "s0", "s1", "t0", "t1")


def gelu_pair(p):
    s = jnp.tanh(ROOT * (p + CUBIC * p * p * p))
    value = 0.5 * p * (1.0 + s)
    slope = 0.5 * (1.0 + s) + 0.5 * p * (1.0 - s * s) * ROOT * (1.0 + 3.0 * CUBIC * p * p)
    return value, slope


def dot(a, b):
    return jnp.dot(a, b, preferred_element_type=F32)


def dot_nt(a, b):
    return lax.dot_general(a, b, (((1,), (1,)), ((), ())), preferred_element_type=F32)


def dot_tn(a, b):
    return lax.dot_general(a, b, (((0,), (0,)), ((), ())), preferred_element_type=F32)


def kernel(
    c1, c2,
    tok_ref, cot_ref, gate_ref, ecol_ref, erow_ref, pack_ref, spread_ref, win_hbm, wout_hbm,
    out_ref, gin_hbm, gout_hbm,
    sx1, sx2, sc1, sc2, ax1, ax2, ac1, ac2,
    gx1, gx2, gc1, gc2,
    win, wout, hid, slp, bh, p1, p2,
    ra, rb, rc, rd, rz, q1, qs0, qs1, qt0, qt1, zout,
    ret1, ret2, back1, back2,
    wsem, a_send, a_recv, g_send, g_recv, r_send, r_recv,
):
    e = lax.axis_index("expert")
    d = lax.axis_index("dp")
    zhi = e // 8
    x = d // 2
    zlo = d % 2
    zot = 1 - zlo
    xr = (x + 1) % NX
    xl = (x + 3) % NX
    xf = (x + 2) % NX
    zp = x * 2 + zot
    dxr = xr * 2 + zlo
    dxl = xl * 2 + zlo
    right, left, pair = (e, dxr), (e, dxl), (e, zp)

    def group_dev(g):
        cross = (zhi + g // 8) % 2
        return (g, x * 2 + (zlo + cross) % 2)

    load_in = pltpu.make_async_copy(win_hbm, win, wsem.at[0])
    load_out = pltpu.make_async_copy(wout_hbm, wout, wsem.at[1])
    load_in.start()
    load_out.start()

    bar = pltpu.get_barrier_semaphore()

    def greet(k, carry):
        pl.semaphore_signal(bar, inc=1, device_id=group_dev((e + k) % NG), device_id_type=MESH)
        return carry

    lax.fori_loop(1, NG, greet, 0)
    for dev in (right, left, pair):
        pl.semaphore_signal(bar, inc=1, device_id=dev, device_id_type=MESH)

    n_tok = tok_ref.shape[0]
    n_exp = NG * LOCAL
    erow = erow_ref[...]
    one_row = (lax.broadcasted_iota(jnp.int32, (n_exp, n_tok), 0) == erow).astype(F32)
    before_row = (
        lax.broadcasted_iota(jnp.int32, (n_tok, n_tok), 0)
        < lax.broadcasted_iota(jnp.int32, (n_tok, n_tok), 1)
    ).astype(F32)
    rank_row = jnp.sum(dot(one_row.astype(BF), before_row.astype(BF)) * one_row, axis=0, keepdims=True)
    slot_row = (erow >> 1) * SLOT + (erow & 1) * CAP + rank_row.astype(jnp.int32)
    ecol = ecol_ref[...]
    one_col = (lax.broadcasted_iota(jnp.int32, (n_tok, n_exp), 1) == ecol).astype(F32)
    before_col = (
        lax.broadcasted_iota(jnp.int32, (n_tok, n_tok), 1)
        < lax.broadcasted_iota(jnp.int32, (n_tok, n_tok), 0)
    ).astype(F32)
    rank_col = jnp.sum(dot(before_col.astype(BF), one_col.astype(BF)) * one_col, axis=1, keepdims=True)
    slot_col = (ecol >> 1) * SLOT + (ecol & 1) * CAP + rank_col.astype(jnp.int32)
    n_slot = NG * SLOT
    put = (lax.broadcasted_iota(jnp.int32, (n_slot, n_tok), 0) == slot_row).astype(F32).astype(BF)

    def fill(dst, acc_dst, value):
        dst[...] = value.astype(BF).reshape(dst.shape)
        acc_dst[pl.ds(e, 1)] = dst[pl.ds(e, 1)]

    def scatter_out(j, src, dst):
        def go(k, carry):
            g = (e + k) % NG
            pltpu.make_async_remote_copy(
                src_ref=src.at[g], dst_ref=dst.at[e], send_sem=a_send.at[j, k], recv_sem=a_recv.at[j, k],
                device_id=group_dev(g), device_id_type=MESH,
            ).start()
            return carry

        lax.fori_loop(1, NG, go, 0)

    def scatter_in(j, src, dst):
        def go(k, carry):
            g = (e + NG - k) % NG
            pltpu.make_async_remote_copy(
                src_ref=src.at[g], dst_ref=dst.at[g], send_sem=a_send.at[j, k], recv_sem=a_recv.at[j, k],
                device_id=group_dev(g), device_id_type=MESH,
            ).wait_recv()
            return carry

        lax.fori_loop(1, NG, go, 0)

    def scatter_sent(j, src, dst):
        def go(k, carry):
            g = (e + k) % NG
            pltpu.make_async_remote_copy(
                src_ref=src.at[g], dst_ref=dst.at[e], send_sem=a_send.at[j, k], recv_sem=a_recv.at[j, k],
                device_id=group_dev(g), device_id_type=MESH,
            ).wait_send()
            return carry

        lax.fori_loop(1, NG, go, 0)

    fill(sx1, ax1, dot(put, tok_ref[:, :c1]))
    pl.semaphore_wait(bar, NG - 1 + 3)
    scatter_out(0, sx1, ax1)
    fill(sx2, ax2, dot(put, tok_ref[:, c1:]))
    scatter_out(1, sx2, ax2)
    gate = gate_ref[...]
    fill(sc1, ac1, dot(put, (gate * cot_ref[:, :c1].astype(F32)).astype(BF)))
    scatter_out(2, sc1, ac1)
    fill(sc2, ac2, dot(put, (gate * cot_ref[:, c1:].astype(F32)).astype(BF)))
    scatter_out(3, sc2, ac2)

    pack = pack_ref[...]

    def compact(j, src, arrived, g):
        scatter_in(j, src, arrived)
        rows = arrived[...].reshape(n_slot, arrived.shape[-1])
        g[pl.ds(d, 1)] = dot(pack, rows).astype(BF).reshape(1, ROWS, arrived.shape[-1])

    sent = []

    def go(sems, names, name, src, dst, dev):
        i = names.index(name)
        cp = pltpu.make_async_remote_copy(
            src_ref=src, dst_ref=dst, send_sem=sems[0].at[i], recv_sem=sems[1].at[i], device_id=dev, device_id_type=MESH
        )
        cp.start()
        sent.append(cp)

    def got(sems, names, name, dst):
        i = names.index(name)
        pltpu.make_async_remote_copy(
            src_ref=dst, dst_ref=dst, send_sem=sems[0].at[i], recv_sem=sems[1].at[i], device_id=pair, device_id_type=MESH
        ).wait_recv()

    lo, hi = pl.ds(0, HALF), pl.ds(HALF, HALF)

    class Gather:
        def __init__(self, i, g1, g2):
            self.sems = (g_send.at[i], g_recv.at[i])
            self.g1, self.g2 = g1, g2

        def go(self, name, ref, dev):
            go(self.sems, AG, name, ref, ref, dev)

        def got(self, name, ref):
            got(self.sems, AG, name, ref)

        def own1(self):
            g1 = self.g1
            self.go("z1", g1.at[d], pair)
            self.go("xp1", g1.at[d], right)
            self.go("xm1", g1.at[d], left)

        def own2(self):
            g2 = self.g2
            self.go("xp2", g2.at[d], right)
            self.go("xm2", g2.at[d], left)
            self.go("z20", g2.at[d], pair)

        def first(self):
            g1 = self.g1
            self.got("z1", g1.at[zp])
            self.go("xp1z", g1.at[zp], right)
            self.go("xm1z", g1.at[zp], left)
            self.got("xp1", g1.at[dxl])
            self.go("fp1", g1.at[dxl, lo], right)
            self.got("xm1", g1.at[dxr])
            self.go("fm1", g1.at[dxr, hi], left)

        def second(self):
            g2 = self.g2
            self.got("xp2", g2.at[dxl])
            self.go("fp2", g2.at[dxl, lo], right)
            self.go("z2m", g2.at[dxl], pair)
            self.got("xm2", g2.at[dxr])
            self.go("fm2", g2.at[dxr, hi], left)
            self.go("z2p", g2.at[dxr], pair)

        def near(self):
            self.got("z20", self.g2.at[zp])

        def third(self):
            g1 = self.g1
            self.got("xp1z", g1.at[xl * 2 + zot])
            self.go("fp1z", g1.at[xl * 2 + zot, lo], right)
            self.got("xm1z", g1.at[xr * 2 + zot])
            self.go("fm1z", g1.at[xr * 2 + zot, hi], left)

        def fourth(self):
            g2 = self.g2
            self.got("fp2", g2.at[xf * 2 + zlo, lo])
            self.got("fm2", g2.at[xf * 2 + zlo, hi])
            self.go("z22", g2.at[xf * 2 + zlo], pair)

        def left_done(self):
            self.got("z2m", self.g2.at[xl * 2 + zot])

        def right_done(self):
            self.got("z2p", self.g2.at[xr * 2 + zot])

        def far_done(self):
            g1 = self.g1
            self.got("fp1", g1.at[xf * 2 + zlo, lo])
            self.got("fm1", g1.at[xf * 2 + zlo, hi])
            self.got("fp1z", g1.at[xf * 2 + zot, lo])
            self.got("fm1z", g1.at[xf * 2 + zot, hi])
            self.got("z22", self.g2.at[xf * 2 + zot])

    def block(ref, xi, le):
        return ref[pl.ds(2 * xi, 2), pl.ds(pl.multiple_of(le * HALF, 32), HALF), :].reshape(2 * HALF, ref.shape[-1])

    def keep(ref, xi, le, value):
        ref[pl.ds(2 * xi, 2), pl.ds(pl.multiple_of(le * HALF, 32), HALF), :] = value.reshape(2, HALF, ref.shape[-1])

    def forward(xi):
        def one(le, carry):
            pre = dot(block(gx1, xi, le), win[le, :c1, :]) + dot(block(gx2, xi, le), win[le, c1:, :])
            value, slope = gelu_pair(pre)
            h = value.astype(BF)
            keep(hid, xi, le, h)
            keep(slp, xi, le, slope)
            keep(p1, xi, le, dot(h, wout[le, :, :c1]).astype(BF))
            keep(p2, xi, le, dot(h, wout[le, :, c1:]).astype(BF))
            return carry

        lax.fori_loop(0, LOCAL, one, 0)

    def backward(xi):
        def one(le, carry):
            b = dot_nt(block(gc1, xi, le), wout[le, :, :c1]) + dot_nt(block(gc2, xi, le), wout[le, :, c1:])
            keep(bh, xi, le, (b * block(slp, xi, le)).astype(BF))
            return carry

        lax.fori_loop(0, LOCAL, one, 0)

    def rows_of(ref, le, start, size):
        return ref[:, pl.ds(pl.multiple_of(le * HALF, 32), HALF), pl.ds(start, size)].reshape(ND * HALF, size)

    TILE = 128

    def grads_in(le):
        bhe = rows_of(bh, le, 0, bh.shape[-1])

        def first(i, carry):
            s = pl.multiple_of(i * TILE, TILE)
            win[le, pl.ds(s, TILE), :] = dot_tn(rows_of(gx1, le, s, TILE), bhe).astype(BF)
            return carry

        def second(i, carry):
            s = pl.multiple_of(i * TILE, TILE)
            win[le, pl.ds(c1 + s, TILE), :] = dot_tn(rows_of(gx2, le, s, TILE), bhe).astype(BF)
            return carry

        lax.fori_loop(0, c1 // TILE, first, 0)
        lax.fori_loop(0, c2 // TILE, second, 0)

    def grads_out(le):
        def one(i, carry):
            s = pl.multiple_of(i * TILE, TILE)
            h = rows_of(hid, le, s, TILE)
            wout[le, pl.ds(s, TILE), :c1] = dot_tn(h, rows_of(gc1, le, 0, c1)).astype(BF)
            wout[le, pl.ds(s, TILE), c1:] = dot_tn(h, rows_of(gc2, le, 0, c2)).astype(BF)
            return carry

        lax.fori_loop(0, hid.shape[-1] // TILE, one, 0)

    rsems = (r_send, r_recv)

    def rgo(name, src, dst, dev):
        go(rsems, RS, name, src, dst, dev)

    def rgot(name, dst):
        got(rsems, RS, name, dst)

    def add(dst, src):
        dst[...] = (dst[...].astype(F32) + src[...].astype(F32)).astype(BF)

    zs = ((0, zlo), (1, zot))

    X, C = Gather(0, gx1, gx2), Gather(1, gc1, gc2)
    compact(0, sx1, ax1, gx1)
    X.own1()
    compact(1, sx2, ax2, gx2)
    X.own2()
    compact(2, sc1, ac1, gc1)
    compact(3, sc2, ac2, gc2)
    X.first()
    X.second()
    X.near()
    load_in.wait()
    load_out.wait()
    forward(x)
    C.own1()
    C.own2()
    X.third()
    X.fourth()
    X.left_done()
    forward(xl)
    X.right_done()
    forward(xr)
    C.first()
    C.second()
    X.far_done()
    forward(xf)
    for j, z in zs:
        rgo(f"a{j}", p1.at[xf * 2 + z, lo], ra.at[j], right)
        rgo(f"b{j}", p1.at[xf * 2 + z, hi], rb.at[j], left)
    for j, xi in enumerate((xf, xl, xr, x)):
        rgo(f"q{j}", p2.at[xi * 2 + zot], q1.at[j], pair)
    C.near()
    backward(x)
    C.third()
    C.fourth()
    C.left_done()
    backward(xl)
    C.right_done()
    backward(xr)
    for j, z in zs:
        rgot(f"a{j}", ra.at[j])
        add(p1.at[xr * 2 + z, lo], ra.at[j])
        rgo(f"c{j}", p1.at[xr * 2 + z], rc.at[j], right)
        rgot(f"b{j}", rb.at[j])
        add(p1.at[xl * 2 + z, hi], rb.at[j])
        rgo(f"d{j}", p1.at[xl * 2 + z], rd.at[j], left)
    for j, xi in enumerate((xf, xl, xr, x)):
        rgot(f"q{j}", q1.at[j])
        add(p2.at[xi * 2 + zlo], q1.at[j])
        if j == 0:
            rgo("s0", p2.at[xf * 2 + zlo, lo], qs0, right)
            rgo("s1", p2.at[xf * 2 + zlo, hi], qs1, left)
    C.far_done()
    backward(xf)
    grads_in(0)
    rgot("s0", qs0)
    add(p2.at[xr * 2 + zlo, lo], qs0)
    rgo("t0", p2.at[xr * 2 + zlo], qt0, right)
    rgot("s1", qs1)
    add(p2.at[xl * 2 + zlo, hi], qs1)
    rgo("t1", p2.at[xl * 2 + zlo], qt1, left)
    rgot("c1", rc.at[1])
    rgot("d1", rd.at[1])
    zout[...] = (p1[zp].astype(F32) + rc[1].astype(F32) + rd[1].astype(F32)).astype(BF)
    rgo("z", zout, rz, pair)
    grads_in(1)
    save_in = pltpu.make_async_copy(win, gin_hbm, wsem.at[0])
    save_in.start()
    grads_out(0)
    grads_out(1)
    save_out = pltpu.make_async_copy(wout, gout_hbm, wsem.at[1])
    save_out.start()
    spread = spread_ref[...]
    rgot("t0", qt0)
    rgot("t1", qt1)
    total = p2[d].astype(F32) + qt0[...].astype(F32) + qt1[...].astype(F32)
    fill(ret2, back2, dot(spread, total.astype(BF)))
    scatter_out(4, ret2, back2)
    rgot("c0", rc.at[0])
    rgot("d0", rd.at[0])
    rgot("z", rz)
    total = p1[d].astype(F32) + rc[0].astype(F32) + rd[0].astype(F32) + rz[...].astype(F32)
    fill(ret1, back1, dot(spread, total.astype(BF)))
    scatter_out(5, ret1, back1)
    take = (lax.broadcasted_iota(jnp.int32, (n_tok, n_slot), 1) == slot_col).astype(F32).astype(BF)
    scatter_in(4, ret2, back2)
    out_ref[:, c1:] = (gate * dot(take, back2[...].reshape(n_slot, c2))).astype(BF)
    scatter_in(5, ret1, back1)
    out_ref[:, :c1] = (gate * dot(take, back1[...].reshape(n_slot, c1))).astype(BF)

    for j, (src, dst) in enumerate(((sx1, ax1), (sx2, ax2), (sc1, ac1), (sc2, ac2), (ret2, back2), (ret1, back1))):
        scatter_sent(j, src, dst)
    for cp in sent:
        cp.wait_send()
    save_in.wait()
    save_out.wait()


def shards(tokens, cotangent, gate_prob, expert_of, w_in, w_out):
    n_tok, width = tokens.shape
    ff = w_in.shape[-1]
    c1 = width * 9 // 16
    c2 = width - c1
    o = np.arange(ROWS)
    source = (o % HALF) // CAP * SLOT + o // HALF * CAP + o % CAP
    pack = (np.arange(NG * SLOT)[None, :] == source[:, None]).astype(np.float32)
    vm = pl.BlockSpec(memory_space=pltpu.VMEM)
    hbm = pl.BlockSpec(memory_space=pl.ANY)

    def buf(*shape):
        return pltpu.VMEM(shape, BF)

    slots = [buf(NG, SLOT, c1), buf(NG, SLOT, c2)]
    gathered = [buf(ND, ROWS, c1), buf(ND, ROWS, c2)]
    return pl.pallas_call(
        functools.partial(kernel, c1, c2),
        out_shape=(
            jax.ShapeDtypeStruct(tokens.shape, BF),
            jax.ShapeDtypeStruct(w_in.shape, BF),
            jax.ShapeDtypeStruct(w_out.shape, BF),
        ),
        in_specs=[vm] * 7 + [hbm] * 2,
        out_specs=(vm, hbm, hbm),
        scratch_shapes=[
            *slots, *slots, *slots, *slots,
            *gathered, *gathered,
            buf(*w_in.shape), buf(*w_out.shape),
            buf(ND, ROWS, ff), pltpu.VMEM((ND, ROWS, ff), F32), buf(ND, ROWS, ff),
            *gathered,
            buf(2, HALF, c1), buf(2, HALF, c1), buf(2, ROWS, c1), buf(2, ROWS, c1), buf(ROWS, c1),
            buf(NX, ROWS, c2), buf(HALF, c2), buf(HALF, c2), buf(ROWS, c2), buf(ROWS, c2), buf(ROWS, c1),
            *slots, *slots,
            pltpu.SemaphoreType.DMA((2,)),
            pltpu.SemaphoreType.DMA((6, NG)), pltpu.SemaphoreType.DMA((6, NG)),
            pltpu.SemaphoreType.DMA((2, len(AG))), pltpu.SemaphoreType.DMA((2, len(AG))),
            pltpu.SemaphoreType.DMA((len(RS),)), pltpu.SemaphoreType.DMA((len(RS),)),
        ],
        compiler_params=pltpu.CompilerParams(collective_id=0, has_side_effects=True, vmem_limit_bytes=62 << 20),
        cost_estimate=pl.CostEstimate(
            flops=10 * ND * ROWS * width * ff, bytes_accessed=8 * w_in.size, transcendentals=ND * ROWS * ff
        ),
    )(
        tokens, cotangent, gate_prob[:, None], expert_of, expert_of.reshape(1, n_tok),
        jnp.asarray(pack, BF), jnp.asarray(pack.T, BF), w_in, w_out,
    )


def solution(mesh):
    return jax.shard_map(
        shards,
        mesh=mesh,
        in_specs=(
            P(("expert", "dp"), None),
            P(("expert", "dp"), None),
            P(("expert", "dp")),
            P(("expert", "dp"), None),
            P("expert", None, "dp"),
            P("expert", "dp", None),
        ),
        out_specs=(P(("expert", "dp"), None), P("expert", None, "dp"), P("expert", "dp", None)),
        check_vma=False,
    )
```

```python
import functools

import jax
import jax.numpy as jnp
import numpy as np
from jax import lax
from jax.experimental import pallas as pl
from jax.experimental.pallas import tpu as pltpu
from jax.sharding import PartitionSpec as P

ROOT = 0.7978845608028654
CUBIC = 0.044715
BF = jnp.bfloat16
F32 = jnp.float32
MESH = pl.DeviceIdType.MESH
CAP = 6
LOCAL = 2
SLOT = 16
NG = 16
NX = 4
ND = 8
HALF = NG * CAP
ROWS = LOCAL * HALF

ARRAY = ("rz", "rr", "rl", "hr", "hl", "xp1", "xm1", "xp1z", "xm1z", "fp1", "fm1", "fp1z", "fm1z", "z20", "z2m", "z2p", "z22")
BACK = ("a0", "a1", "b0", "b1", "c0", "c1", "d0", "d1", "q0", "q1", "q2", "q3", "s0", "s1", "t0", "t1", "z")
NAMES = (
    *("x" + n for n in ARRAY), *("c" + n for n in ARRAY), *("b" + n for n in BACK), "iz", "ir", "il", "if"
)


def gelu_pair(p):
    s = jnp.tanh(ROOT * (p + CUBIC * p * p * p))
    value = 0.5 * p * (1.0 + s)
    slope = 0.5 * (1.0 + s) + 0.5 * p * (1.0 - s * s) * ROOT * (1.0 + 3.0 * CUBIC * p * p)
    return value, slope


def dot(a, b):
    return jnp.dot(a, b, preferred_element_type=F32)


def dot_nt(a, b):
    return lax.dot_general(a, b, (((1,), (1,)), ((), ())), preferred_element_type=F32)


def dot_tn(a, b):
    return lax.dot_general(a, b, (((0,), (0,)), ((), ())), preferred_element_type=F32)


def kernel(
    c1, c2,
    tok_ref, cot_ref, gate_ref, erow_ref, pack_ref, spread_ref, win_hbm, wout_hbm,
    out_ref, win, wout,
    slots, u1, u2, v1, v2, s7, s6, x7, x6, y7, y6, b7, b6,
    gx1, gx2, gc1, gc2, hid, bh, p1, p2,
    ra, rb, rc, rd, rz, q1, qs0, qs1, qt0, qt1, w1, w2,
    wsem, a_send, a_recv, n_send, n_recv,
):
    e = lax.axis_index("expert")
    d = lax.axis_index("dp")
    zhi = e // 8
    x = d // 2
    zlo = d % 2
    zot = 1 - zlo
    xr = (x + 1) % NX
    xl = (x + 3) % NX
    xf = (x + 2) % NX
    zp = x * 2 + zot
    dxr = xr * 2 + zlo
    dxl = xl * 2 + zlo
    dxf = xf * 2 + zlo
    right, left, pair, far = (e, dxr), (e, dxl), (e, zp), (e, dxf)
    n_tok, width = tok_ref.shape
    n_exp = NG * LOCAL
    n_slot = NG * SLOT

    def group_dev(g):
        cross = (zhi + g // 8) % 2
        return (g, x * 2 + (zlo + cross) % 2)

    bar = pltpu.get_barrier_semaphore()

    def greet(k, carry):
        pl.semaphore_signal(bar, inc=1, device_id=group_dev((e + k) % NG), device_id_type=MESH)
        return carry

    for dev in (right, left, pair, far):
        pl.semaphore_signal(bar, inc=1, device_id=dev, device_id_type=MESH)
    lax.fori_loop(1, NG, greet, 0)

    load_in = pltpu.make_async_copy(win_hbm, win, wsem.at[0])
    load_out = pltpu.make_async_copy(wout_hbm, wout, wsem.at[1])
    load_in.start()
    load_out.start()

    erow = erow_ref[...]
    one_row = (lax.broadcasted_iota(jnp.int32, (n_exp, n_tok), 0) == erow).astype(F32)
    before = (
        lax.broadcasted_iota(jnp.int32, (n_tok, n_tok), 0)
        < lax.broadcasted_iota(jnp.int32, (n_tok, n_tok), 1)
    ).astype(F32)
    rank = jnp.sum(dot(one_row.astype(BF), before.astype(BF)) * one_row, axis=0, keepdims=True)
    slot_row = (erow >> 1) * SLOT + (erow & 1) * CAP + rank.astype(jnp.int32)
    slots[pl.ds(d, 1)] = jnp.broadcast_to(slot_row, (8, n_tok)).reshape(1, 8, n_tok)
    eye = lax.broadcasted_iota(jnp.int32, (n_tok, n_tok), 0) == lax.broadcasted_iota(jnp.int32, (n_tok, n_tok), 1)

    def column(row):
        return jnp.sum(jnp.where(eye, row, jnp.zeros_like(row)), axis=1, keepdims=True)

    def put(b):
        row = slots[b][:1]
        return (lax.broadcasted_iota(jnp.int32, (n_slot, n_tok), 0) == row).astype(F32).astype(BF)

    def take(b):
        col = column(slots[b][:1])
        return (lax.broadcasted_iota(jnp.int32, (n_tok, n_slot), 1) == col).astype(F32).astype(BF)

    gate = column(gate_ref[...])
    u1[pl.ds(zlo, 1)] = tok_ref[:, :c1].reshape(1, n_tok, c1)
    u2[pl.ds(x, 1)] = tok_ref[:, c1:].reshape(1, n_tok, c2)
    v1[pl.ds(zlo, 1)] = (gate * cot_ref[:, :c1].astype(F32)).astype(BF).reshape(1, n_tok, c1)
    v2[pl.ds(x, 1)] = (gate * cot_ref[:, c1:].astype(F32)).astype(BF).reshape(1, n_tok, c2)

    sent = []

    def go(name, src, dst, dev):
        i = NAMES.index(name)
        cp = pltpu.make_async_remote_copy(
            src_ref=src, dst_ref=dst, send_sem=n_send.at[i], recv_sem=n_recv.at[i], device_id=dev, device_id_type=MESH
        )
        cp.start()
        sent.append(cp)

    def got(name, dst):
        i = NAMES.index(name)
        pltpu.make_async_remote_copy(
            src_ref=dst, dst_ref=dst, send_sem=n_send.at[i], recv_sem=n_recv.at[i], device_id=pair, device_id_type=MESH
        ).wait_recv()

    def across(j, src, dst):
        return pltpu.make_async_remote_copy(
            src_ref=src, dst_ref=dst, send_sem=a_send.at[j], recv_sem=a_recv.at[j], device_id=pair, device_id_type=MESH
        )

    def scatter_out(j, src, dst, value):
        src[...] = value.astype(BF).reshape(src.shape)
        dst[pl.ds(e, 1)] = src[pl.ds(e, 1)]

        def one(k, carry):
            g = (e + k) % NG
            pltpu.make_async_remote_copy(
                src_ref=src.at[g], dst_ref=dst.at[e], send_sem=a_send.at[j], recv_sem=a_recv.at[j],
                device_id=group_dev(g), device_id_type=MESH,
            ).start()
            return carry

        lax.fori_loop(1, NG, one, 0)

    others = pl.ds(0, NG - 1)

    def scatter_in(j, src, dst):
        across(j, src.at[others], dst.at[others]).wait_recv()
        return dst[...].reshape(n_slot, dst.shape[-1])

    def scatter_sent(j, src, dst):
        across(j, src.at[others], dst.at[others]).wait_send()

    lo, hi = pl.ds(0, HALF), pl.ds(HALF, HALF)
    tlo, thi = pl.ds(0, n_tok // 2), pl.ds(n_tok // 2, n_tok // 2)
    row_x = (x, xl, xr, xf)

    class Array:
        def __init__(self, i, tag, raw1, raw2, a7, a6, g1, g2):
            self.i, self.tag = i, tag
            self.raw1, self.raw2, self.a7, self.a6, self.g1, self.g2 = raw1, raw2, a7, a6, g1, g2

        def go(self, name, ref, dev):
            go(self.tag + name, ref, ref, dev)

        def got(self, name, ref):
            got(self.tag + name, ref)

        def raw(self):
            self.go("rr", self.raw2.at[x], right)
            self.go("rl", self.raw2.at[x], left)
            self.go("rz", self.raw1.at[zlo], pair)

        def free(self, b):
            if self.i > 0:
                scatter_sent(6 * self.i - 6 + b, s7.at[b] if b < 2 else s6.at[b - 2], b7.at[b] if b < 2 else b6.at[b - 2])

        def own1(self):
            self.free(0)
            scatter_out(6 * self.i, s7.at[0], self.a7.at[0], dot(put(d), self.raw1[zlo]))

        def own2(self):
            self.free(2)
            scatter_out(6 * self.i + 2, s6.at[0], self.a6.at[0], dot(put(d), self.raw2[x]))

        def pair1(self):
            self.got("rz", self.raw1.at[zot])
            self.free(1)
            scatter_out(6 * self.i + 1, s7.at[1], self.a7.at[1], dot(put(zp), self.raw1[zot]))

        def pass_on(self):
            self.got("rr", self.raw2.at[xl])
            self.go("hr", self.raw2.at[xl, tlo], right)
            self.got("rl", self.raw2.at[xr])
            self.go("hl", self.raw2.at[xr, thi], left)

        def near2(self):
            for b, xi in ((1, xl), (2, xr)):
                self.free(2 + b)
                scatter_out(6 * self.i + 2 + b, s6.at[b], self.a6.at[b], dot(put(xi * 2 + zlo), self.raw2[xi]))

        def far2(self):
            self.got("hr", self.raw2.at[xf, tlo])
            self.got("hl", self.raw2.at[xf, thi])
            self.free(5)
            scatter_out(6 * self.i + 5, s6.at[3], self.a6.at[3], dot(put(dxf), self.raw2[xf]))

        def land1(self, b):
            rows = scatter_in(6 * self.i + b, s7.at[b], self.a7.at[b])
            at = (d, zp)[b]
            self.g1[pl.ds(at, 1)] = dot(pack_ref[...], rows).astype(BF).reshape(1, ROWS, c1)
            self.go(("xp1", "xp1z")[b], self.g1.at[at], right)
            self.go(("xm1", "xm1z")[b], self.g1.at[at], left)

        def land2(self, b):
            rows = scatter_in(6 * self.i + 2 + b, s6.at[b], self.a6.at[b])
            at = row_x[b] * 2 + zlo
            self.g2[pl.ds(at, 1)] = dot(pack_ref[...], rows).astype(BF).reshape(1, ROWS, c2)
            self.go(("z20", "z2m", "z2p", "z22")[b], self.g2.at[at], pair)

        def ring(self, b):
            g1, z, t = self.g1, (zlo, zot)[b], ("", "z")[b]
            self.got("xp1" + t, g1.at[xl * 2 + z])
            self.go("fp1" + t, g1.at[xl * 2 + z, lo], right)
            self.got("xm1" + t, g1.at[xr * 2 + z])
            self.go("fm1" + t, g1.at[xr * 2 + z, hi], left)

        def whole(self, b):
            if b == 3:
                for z, t in ((zlo, ""), (zot, "z")):
                    self.got("fp1" + t, self.g1.at[xf * 2 + z, lo])
                    self.got("fm1" + t, self.g1.at[xf * 2 + z, hi])
            self.got(("z20", "z2m", "z2p", "z22")[b], self.g2.at[row_x[b] * 2 + zot])

    def block(ref, xi, le):
        return ref[pl.ds(2 * xi, 2), pl.ds(pl.multiple_of(le * HALF, 32), HALF), :].reshape(2 * HALF, ref.shape[-1])

    def keep(ref, xi, le, value):
        ref[pl.ds(2 * xi, 2), pl.ds(pl.multiple_of(le * HALF, 32), HALF), :] = value.reshape(2, HALF, ref.shape[-1])

    def forward(xi):
        def one(le, carry):
            pre = dot(block(gx1, xi, le), win[le, :c1, :]) + dot(block(gx2, xi, le), win[le, c1:, :])
            value, slope = gelu_pair(pre)
            h = value.astype(BF)
            keep(hid, xi, le, h)
            keep(bh, xi, le, slope.astype(BF))
            keep(p1, xi, le, dot(h, wout[le, :, :c1]).astype(BF))
            keep(p2, xi, le, dot(h, wout[le, :, c1:]).astype(BF))
            return carry

        lax.fori_loop(0, LOCAL, one, 0)

    def backward(xi):
        def one(le, carry):
            b = dot_nt(block(gc1, xi, le), wout[le, :, :c1]) + dot_nt(block(gc2, xi, le), wout[le, :, c1:])
            keep(bh, xi, le, (b * block(bh, xi, le).astype(F32)).astype(BF))
            return carry

        lax.fori_loop(0, LOCAL, one, 0)

    def rows_of(ref, le, start, size):
        return ref[:, pl.ds(pl.multiple_of(le * HALF, 32), HALF), pl.ds(start, size)].reshape(ND * HALF, size)

    TILE = 128

    def grads_in(le):
        bhe = rows_of(bh, le, 0, bh.shape[-1])

        def first(i, carry):
            s = pl.multiple_of(i * (c1 // 3), TILE)
            win[le, pl.ds(s, c1 // 3), :] = dot_tn(rows_of(gx1, le, s, c1 // 3), bhe).astype(BF)
            return carry

        lax.fori_loop(0, 3, first, 0)
        win[le, c1:, :] = dot_tn(rows_of(gx2, le, 0, c2), bhe).astype(BF)

    def grads_out(le):
        def one(i, carry):
            s = pl.multiple_of(i * TILE, TILE)
            h = rows_of(hid, le, s, TILE)
            wout[le, pl.ds(s, TILE), :c1] = dot_tn(h, rows_of(gc1, le, 0, c1)).astype(BF)
            wout[le, pl.ds(s, TILE), c1:] = dot_tn(h, rows_of(gc2, le, 0, c2)).astype(BF)
            return carry

        lax.fori_loop(0, hid.shape[-1] // TILE, one, 0)

    def add(dst, src):
        dst[...] = (dst[...].astype(F32) + src[...].astype(F32)).astype(BF)

    zs = ((0, zlo), (1, zot))
    order = ((3, xf), (1, xl), (2, xr), (0, x))

    def back_first():
        for j, z in zs[::-1]:
            go(f"ba{j}", p1.at[xf * 2 + z, lo], ra.at[j], right)
            go(f"bb{j}", p1.at[xf * 2 + z, hi], rb.at[j], left)

    def back_pair(b, xi):
        go(f"bq{b}", p2.at[xi * 2 + zot], q1.at[b], pair)

    def back_second(j):
        z = (zlo, zot)[j]
        got(f"ba{j}", ra.at[j])
        add(p1.at[xr * 2 + z, lo], ra.at[j])
        go(f"bc{j}", p1.at[xr * 2 + z], rc.at[j], right)
        got(f"bb{j}", rb.at[j])
        add(p1.at[xl * 2 + z, hi], rb.at[j])
        go(f"bd{j}", p1.at[xl * 2 + z], rd.at[j], left)

    def back_third(j):
        got(f"bc{j}", rc.at[j])
        got(f"bd{j}", rd.at[j])
        total = p1[(d, zp)[j]].astype(F32) + rc[j].astype(F32) + rd[j].astype(F32)
        scatter_sent(6 + j, s7.at[j], y7.at[j])
        scatter_out(12 + j, s7.at[j], b7.at[j], dot(spread_ref[...], total.astype(BF)))

    def back_across(b, xi):
        got(f"bq{b}", q1.at[b])
        total = p2[xi * 2 + zlo].astype(F32) + q1[b].astype(F32)
        scatter_sent(8 + b, s6.at[b], y6.at[b])
        scatter_out(14 + b, s6.at[b], b6.at[b], dot(spread_ref[...], total.astype(BF)))

    def rows_back(b, at):
        if b < 2:
            return dot(take(at), scatter_in(12 + b, s7.at[b], b7.at[b]))
        return dot(take(at), scatter_in(12 + b, s6.at[b - 2], b6.at[b - 2]))

    def back_far():
        w2[0] = rows_back(5, dxf).astype(BF)
        go("bs0", w2.at[0, tlo], qs0, right)
        go("bs1", w2.at[0, thi], qs1, left)

    def back_near():
        w2[1] = rows_back(4, dxr).astype(BF)
        w2[2] = rows_back(3, dxl).astype(BF)
        got("bs0", qs0)
        add(w2.at[1, tlo], qs0)
        go("bt0", w2.at[1], qt0, right)
        got("bs1", qs1)
        add(w2.at[2, thi], qs1)
        go("bt1", w2.at[2], qt1, left)

    def back_own():
        mine = rows_back(2, d)
        got("bt0", qt0)
        got("bt1", qt1)
        out_ref[:, c1:] = (gate * (mine + qt0[...].astype(F32) + qt1[...].astype(F32))).astype(BF)

    def back_z():
        w1[...] = rows_back(1, zp).astype(BF)
        go("bz", w1, rz, pair)

    def back_z_own():
        mine = rows_back(0, d)
        got("bz", rz)
        out_ref[:, :c1] = (gate * (mine + rz[...].astype(F32))).astype(BF)

    X = Array(0, "x", u1, u2, x7, x6, gx1, gx2)
    C = Array(1, "c", v1, v2, y7, y6, gc1, gc2)

    pl.semaphore_wait(bar, NG - 1 + 4)
    go("iz", slots.at[d], slots.at[d], pair)
    go("ir", slots.at[d], slots.at[d], right)
    go("il", slots.at[d], slots.at[d], left)
    go("if", slots.at[d], slots.at[d], far)
    X.raw()
    X.own1()
    X.own2()
    C.raw()
    got("iz", slots.at[zp])
    X.pair1()
    got("ir", slots.at[dxl])
    got("il", slots.at[dxr])
    X.pass_on()
    X.near2()
    X.land1(0)
    X.land2(0)
    got("if", slots.at[dxf])
    X.far2()
    C.own1()
    X.land1(1)
    C.pair1()
    C.own2()
    C.pass_on()
    C.near2()
    X.ring(0)
    X.land2(1)
    X.land2(2)
    load_in.wait()
    load_out.wait()
    X.whole(0)
    forward(x)
    X.land2(3)
    C.far2()
    X.ring(1)
    C.land1(0)
    C.land1(1)
    C.land2(0)
    X.whole(1)
    forward(xl)
    X.whole(2)
    forward(xr)
    C.ring(0)
    C.land2(1)
    C.land2(2)
    X.whole(3)
    forward(xf)
    back_first()
    back_pair(*order[0])
    C.land2(3)
    C.ring(1)
    back_pair(*order[1])
    back_pair(*order[2])
    back_pair(*order[3])
    C.whole(0)
    backward(x)
    C.whole(1)
    backward(xl)
    C.whole(2)
    backward(xr)
    back_across(*order[0])
    back_second(1)
    back_second(0)
    C.whole(3)
    backward(xf)
    back_far()
    grads_in(0)
    back_across(*order[1])
    back_third(1)
    back_across(*order[2])
    back_third(0)
    grads_in(1)
    back_near()
    back_across(*order[3])
    back_z()
    grads_out(0)
    grads_out(1)
    back_own()
    back_z_own()

    for b in range(6):
        scatter_sent(12 + b, s7.at[b] if b < 2 else s6.at[b - 2], b7.at[b] if b < 2 else b6.at[b - 2])
    for cp in sent:
        cp.wait_send()


def shards(tokens, cotangent, gate_prob, expert_of, w_in, w_out):
    n_tok, width = tokens.shape
    ff = w_in.shape[-1]
    c1 = width * 9 // 16
    c2 = width - c1
    o = np.arange(ROWS)
    source = (o % HALF) // CAP * SLOT + o // HALF * CAP + o % CAP
    pack = (np.arange(NG * SLOT)[None, :] == source[:, None]).astype(np.float32)
    vm = pl.BlockSpec(memory_space=pltpu.VMEM)
    hbm = pl.BlockSpec(memory_space=pl.ANY)

    def buf(*shape):
        return pltpu.VMEM(shape, BF)

    sevens = [buf(2, NG, SLOT, c1), buf(NX, NG, SLOT, c2)]
    raws = [buf(2, n_tok, c1), buf(NX, n_tok, c2)]
    gathered = [buf(ND, ROWS, c1), buf(ND, ROWS, c2)]
    return pl.pallas_call(
        functools.partial(kernel, c1, c2),
        out_shape=(
            pltpu.VMEM(tokens.shape, BF),
            pltpu.VMEM(w_in.shape, BF),
            pltpu.VMEM(w_out.shape, BF),
        ),
        in_specs=[vm] * 6 + [hbm] * 2,
        out_specs=(vm, vm, vm),
        scratch_shapes=[
            pltpu.VMEM((ND, 8, n_tok), jnp.int32),
            *raws, *raws,
            *sevens, *sevens, *sevens, *sevens,
            *gathered, *gathered,
            buf(ND, ROWS, ff), buf(ND, ROWS, ff),
            *gathered,
            buf(2, HALF, c1), buf(2, HALF, c1), buf(2, ROWS, c1), buf(2, ROWS, c1), buf(n_tok, c1),
            buf(NX, ROWS, c2), buf(n_tok // 2, c2), buf(n_tok // 2, c2), buf(n_tok, c2), buf(n_tok, c2),
            buf(n_tok, c1), buf(3, n_tok, c2),
            pltpu.SemaphoreType.DMA((2,)),
            pltpu.SemaphoreType.DMA((18,)), pltpu.SemaphoreType.DMA((18,)),
            pltpu.SemaphoreType.DMA((len(NAMES),)), pltpu.SemaphoreType.DMA((len(NAMES),)),
        ],
        compiler_params=pltpu.CompilerParams(collective_id=0, has_side_effects=True, vmem_limit_bytes=50 << 20),
        cost_estimate=pl.CostEstimate(
            flops=10 * ND * ROWS * width * ff, bytes_accessed=8 * w_in.size, transcendentals=ND * ROWS * ff
        ),
    )(
        tokens, cotangent, gate_prob.reshape(1, n_tok), expert_of.reshape(1, n_tok),
        jnp.asarray(pack, BF), jnp.asarray(pack.T, BF), w_in, w_out,
    )


def solution(mesh):
    return jax.shard_map(
        shards,
        mesh=mesh,
        in_specs=(
            P(("expert", "dp"), None),
            P(("expert", "dp"), None),
            P(("expert", "dp")),
            P(("expert", "dp"), None),
            P("expert", None, "dp"),
            P("expert", "dp", None),
        ),
        out_specs=(P(("expert", "dp"), None), P("expert", None, "dp"), P("expert", "dp", None)),
        check_vma=False,
    )
```

```python
import functools

import jax
import jax.numpy as jnp
import numpy as np
from jax import lax
from jax.experimental import pallas as pl
from jax.experimental.pallas import tpu as pltpu
from jax.sharding import PartitionSpec as P

ROOT = 0.7978845608028654
CUBIC = 0.044715
BF = jnp.bfloat16
F32 = jnp.float32
MESH = pl.DeviceIdType.MESH
CAP = 6
LOCAL = 2
SLOT = 16
NG = 16
NX = 4
ND = 8
HALF = NG * CAP
ROWS = LOCAL * HALF

ARRAY = ("rz", "rr", "rl", "hr", "hl", "xp1", "xm1", "xp1z", "xm1z", "fp1", "fm1", "fp1z", "fm1z", "z20", "z2m", "z2p", "z22")
BACK = ("a0", "a1", "b0", "b1", "c0", "c1", "d0", "d1", "q0", "q1", "q2", "q3", "s0", "s1", "t0", "t1", "z")
NAMES = (
    *("x" + n for n in ARRAY), *("c" + n for n in ARRAY), *("b" + n for n in BACK), "iz", "ir", "il", "if"
)


def gelu_pair(p):
    s = jnp.tanh(ROOT * (p + CUBIC * p * p * p))
    value = 0.5 * p * (1.0 + s)
    slope = 0.5 * (1.0 + s) + 0.5 * p * (1.0 - s * s) * ROOT * (1.0 + 3.0 * CUBIC * p * p)
    return value, slope


def dot(a, b):
    return jnp.dot(a, b, preferred_element_type=F32)


def dot_nt(a, b):
    return lax.dot_general(a, b, (((1,), (1,)), ((), ())), preferred_element_type=F32)


def dot_tn(a, b):
    return lax.dot_general(a, b, (((0,), (0,)), ((), ())), preferred_element_type=F32)


def kernel(
    c1, c2,
    tok_ref, cot_ref, gate_ref, erow_ref, pack_ref, spread_ref, win_hbm, wout_hbm,
    out_ref, win, wout,
    slots, u1, u2, v1, v2, s7, s6, x7, x6, y7, y6, b7, b6,
    gx1, gx2, gc1, gc2, hid, bh, p1, p2,
    ra, rb, rc, rd, rz, q1, qs0, qs1, qt0, qt1, w1, w2,
    wsem, a_send, a_recv, n_send, n_recv,
):
    e = lax.axis_index("expert")
    d = lax.axis_index("dp")
    zhi = e // 8
    x = d // 2
    zlo = d % 2
    zot = 1 - zlo
    xr = (x + 1) % NX
    xl = (x + 3) % NX
    xf = (x + 2) % NX
    zp = x * 2 + zot
    dxr = xr * 2 + zlo
    dxl = xl * 2 + zlo
    dxf = xf * 2 + zlo
    right, left, pair, far = (e, dxr), (e, dxl), (e, zp), (e, dxf)
    n_tok, width = tok_ref.shape
    n_exp = NG * LOCAL
    n_slot = NG * SLOT

    def group_dev(g):
        cross = (zhi + g // 8) % 2
        return (g, x * 2 + (zlo + cross) % 2)

    bar = pltpu.get_barrier_semaphore()

    def greet(k, carry):
        pl.semaphore_signal(bar, inc=1, device_id=group_dev((e + k) % NG), device_id_type=MESH)
        return carry

    for dev in (right, left, pair, far):
        pl.semaphore_signal(bar, inc=1, device_id=dev, device_id_type=MESH)
    lax.fori_loop(1, NG, greet, 0)

    load_in = pltpu.make_async_copy(win_hbm, win, wsem.at[0])
    load_out = pltpu.make_async_copy(wout_hbm, wout, wsem.at[1])
    load_in.start()
    load_out.start()

    erow = erow_ref[...]
    one_row = (lax.broadcasted_iota(jnp.int32, (n_exp, n_tok), 0) == erow).astype(F32)
    before = (
        lax.broadcasted_iota(jnp.int32, (n_tok, n_tok), 0)
        < lax.broadcasted_iota(jnp.int32, (n_tok, n_tok), 1)
    ).astype(F32)
    rank = jnp.sum(dot(one_row.astype(BF), before.astype(BF)) * one_row, axis=0, keepdims=True)
    slot_row = (erow >> 1) * SLOT + (erow & 1) * CAP + rank.astype(jnp.int32)
    slots[pl.ds(d, 1)] = jnp.broadcast_to(slot_row, (8, n_tok)).reshape(1, 8, n_tok)
    eye = lax.broadcasted_iota(jnp.int32, (n_tok, n_tok), 0) == lax.broadcasted_iota(jnp.int32, (n_tok, n_tok), 1)

    def column(row):
        return jnp.sum(jnp.where(eye, row, jnp.zeros_like(row)), axis=1, keepdims=True)

    def put(b):
        row = slots[b][:1]
        return (lax.broadcasted_iota(jnp.int32, (n_slot, n_tok), 0) == row).astype(F32).astype(BF)

    def take(b):
        col = column(slots[b][:1])
        return (lax.broadcasted_iota(jnp.int32, (n_tok, n_slot), 1) == col).astype(F32).astype(BF)

    gate = column(gate_ref[...])
    u1[pl.ds(zlo, 1)] = tok_ref[:, :c1].reshape(1, n_tok, c1)
    u2[pl.ds(x, 1)] = tok_ref[:, c1:].reshape(1, n_tok, c2)
    v1[pl.ds(zlo, 1)] = (gate * cot_ref[:, :c1].astype(F32)).astype(BF).reshape(1, n_tok, c1)
    v2[pl.ds(x, 1)] = (gate * cot_ref[:, c1:].astype(F32)).astype(BF).reshape(1, n_tok, c2)

    sent = []

    def go(name, src, dst, dev):
        i = NAMES.index(name)
        cp = pltpu.make_async_remote_copy(
            src_ref=src, dst_ref=dst, send_sem=n_send.at[i], recv_sem=n_recv.at[i], device_id=dev, device_id_type=MESH
        )
        cp.start()
        sent.append(cp)

    def got(name, dst):
        i = NAMES.index(name)
        pltpu.make_async_remote_copy(
            src_ref=dst, dst_ref=dst, send_sem=n_send.at[i], recv_sem=n_recv.at[i], device_id=pair, device_id_type=MESH
        ).wait_recv()

    def across(j, src, dst):
        return pltpu.make_async_remote_copy(
            src_ref=src, dst_ref=dst, send_sem=a_send.at[j], recv_sem=a_recv.at[j], device_id=pair, device_id_type=MESH
        )

    def scatter_out(j, src, dst, value):
        src[...] = value.astype(BF).reshape(src.shape)
        dst[pl.ds(e, 1)] = src[pl.ds(e, 1)]

        def one(k, carry):
            g = (e + k) % NG
            pltpu.make_async_remote_copy(
                src_ref=src.at[g], dst_ref=dst.at[e], send_sem=a_send.at[j], recv_sem=a_recv.at[j],
                device_id=group_dev(g), device_id_type=MESH,
            ).start()
            return carry

        lax.fori_loop(1, NG, one, 0)

    others = pl.ds(0, NG - 1)

    def scatter_in(j, src, dst):
        across(j, src.at[others], dst.at[others]).wait_recv()
        return dst[...].reshape(n_slot, dst.shape[-1])

    def scatter_sent(j, src, dst):
        across(j, src.at[others], dst.at[others]).wait_send()

    lo, hi = pl.ds(0, HALF), pl.ds(HALF, HALF)
    tlo, thi = pl.ds(0, n_tok // 2), pl.ds(n_tok // 2, n_tok // 2)
    row_x = (x, xl, xr, xf)

    class Array:
        def __init__(self, i, tag, raw1, raw2, a7, a6, g1, g2):
            self.i, self.tag = i, tag
            self.raw1, self.raw2, self.a7, self.a6, self.g1, self.g2 = raw1, raw2, a7, a6, g1, g2

        def go(self, name, ref, dev):
            go(self.tag + name, ref, ref, dev)

        def got(self, name, ref):
            got(self.tag + name, ref)

        def raw_x(self):
            self.go("rr", self.raw2.at[x], right)
            self.go("rl", self.raw2.at[x], left)

        def raw_z(self):
            self.go("rz", self.raw1.at[zlo], pair)

        def free(self, b):
            if self.i > 0:
                scatter_sent(6 * self.i - 6 + b, s7.at[b] if b < 2 else s6.at[b - 2], b7.at[b] if b < 2 else b6.at[b - 2])

        def own1(self):
            self.free(0)
            scatter_out(6 * self.i, s7.at[0], self.a7.at[0], dot(put(d), self.raw1[zlo]))

        def own2(self):
            self.free(2)
            scatter_out(6 * self.i + 2, s6.at[0], self.a6.at[0], dot(put(d), self.raw2[x]))

        def pair1(self):
            self.got("rz", self.raw1.at[zot])
            self.free(1)
            scatter_out(6 * self.i + 1, s7.at[1], self.a7.at[1], dot(put(zp), self.raw1[zot]))

        def pass_right(self):
            self.got("rr", self.raw2.at[xl])
            self.go("hr", self.raw2.at[xl, tlo], right)

        def pass_left(self):
            self.got("rl", self.raw2.at[xr])
            self.go("hl", self.raw2.at[xr, thi], left)

        def near2(self, b):
            xi = row_x[b]
            self.free(2 + b)
            scatter_out(6 * self.i + 2 + b, s6.at[b], self.a6.at[b], dot(put(xi * 2 + zlo), self.raw2[xi]))

        def far2(self):
            self.got("hr", self.raw2.at[xf, tlo])
            self.got("hl", self.raw2.at[xf, thi])
            self.free(5)
            scatter_out(6 * self.i + 5, s6.at[3], self.a6.at[3], dot(put(dxf), self.raw2[xf]))

        def land1(self, b):
            rows = scatter_in(6 * self.i + b, s7.at[b], self.a7.at[b])
            at = (d, zp)[b]
            self.g1[pl.ds(at, 1)] = dot(pack_ref[...], rows).astype(BF).reshape(1, ROWS, c1)
            self.go(("xp1", "xp1z")[b], self.g1.at[at], right)
            self.go(("xm1", "xm1z")[b], self.g1.at[at], left)

        def land2(self, b):
            rows = scatter_in(6 * self.i + 2 + b, s6.at[b], self.a6.at[b])
            at = row_x[b] * 2 + zlo
            self.g2[pl.ds(at, 1)] = dot(pack_ref[...], rows).astype(BF).reshape(1, ROWS, c2)
            self.go(("z20", "z2m", "z2p", "z22")[b], self.g2.at[at], pair)

        def ring_right(self, b):
            g1, z, t = self.g1, (zlo, zot)[b], ("", "z")[b]
            self.got("xp1" + t, g1.at[xl * 2 + z])
            self.go("fp1" + t, g1.at[xl * 2 + z, lo], right)

        def ring_left(self, b):
            g1, z, t = self.g1, (zlo, zot)[b], ("", "z")[b]
            self.got("xm1" + t, g1.at[xr * 2 + z])
            self.go("fm1" + t, g1.at[xr * 2 + z, hi], left)

        def whole(self, b):
            if b == 3:
                for z, t in ((zlo, ""), (zot, "z")):
                    self.got("fp1" + t, self.g1.at[xf * 2 + z, lo])
                    self.got("fm1" + t, self.g1.at[xf * 2 + z, hi])
            self.got(("z20", "z2m", "z2p", "z22")[b], self.g2.at[row_x[b] * 2 + zot])

    def block(ref, xi, le):
        return ref[pl.ds(2 * xi, 2), pl.ds(pl.multiple_of(le * HALF, 32), HALF), :].reshape(2 * HALF, ref.shape[-1])

    def keep(ref, xi, le, value):
        ref[pl.ds(2 * xi, 2), pl.ds(pl.multiple_of(le * HALF, 32), HALF), :] = value.reshape(2, HALF, ref.shape[-1])

    def forward(xi):
        def one(le, carry):
            pre = dot(block(gx1, xi, le), win[le, :c1, :]) + dot(block(gx2, xi, le), win[le, c1:, :])
            value, slope = gelu_pair(pre)
            h = value.astype(BF)
            keep(hid, xi, le, h)
            keep(bh, xi, le, slope.astype(BF))
            keep(p1, xi, le, dot(h, wout[le, :, :c1]).astype(BF))
            keep(p2, xi, le, dot(h, wout[le, :, c1:]).astype(BF))
            return carry

        lax.fori_loop(0, LOCAL, one, 0)

    def backward(xi):
        def one(le, carry):
            b = dot_nt(block(gc1, xi, le), wout[le, :, :c1]) + dot_nt(block(gc2, xi, le), wout[le, :, c1:])
            keep(bh, xi, le, (b * block(bh, xi, le).astype(F32)).astype(BF))
            return carry

        lax.fori_loop(0, LOCAL, one, 0)

    def rows_of(ref, le, start, size):
        return ref[:, pl.ds(le * HALF, HALF), pl.ds(start, size)].reshape(ND * HALF, size)

    def grads_in(le, part):
        bhe = rows_of(bh, le, 0, bh.shape[-1])
        if part == 0:
            win[le, :c1, :] = dot_tn(rows_of(gx1, le, 0, c1), bhe).astype(BF)
        else:
            win[le, c1:, :] = dot_tn(rows_of(gx2, le, 0, c2), bhe).astype(BF)

    def grads_out(le, part):
        h = rows_of(hid, le, 0, hid.shape[-1])
        if part == 0:
            wout[le, :, :c1] = dot_tn(h, rows_of(gc1, le, 0, c1)).astype(BF)
        else:
            wout[le, :, c1:] = dot_tn(h, rows_of(gc2, le, 0, c2)).astype(BF)

    def add(dst, src):
        dst[...] = (dst[...].astype(F32) + src[...].astype(F32)).astype(BF)

    zs = ((0, zlo), (1, zot))
    def back_first():
        for j, z in zs[::-1]:
            go(f"ba{j}", p1.at[xf * 2 + z, lo], ra.at[j], right)
            go(f"bb{j}", p1.at[xf * 2 + z, hi], rb.at[j], left)

    def back_pair(b):
        xi = row_x[b]
        go(f"bq{b}", p2.at[xi * 2 + zot], q1.at[b], pair)

    def back_second(j):
        z = (zlo, zot)[j]
        got(f"ba{j}", ra.at[j])
        add(p1.at[xr * 2 + z, lo], ra.at[j])
        go(f"bc{j}", p1.at[xr * 2 + z], rc.at[j], right)
        got(f"bb{j}", rb.at[j])
        add(p1.at[xl * 2 + z, hi], rb.at[j])
        go(f"bd{j}", p1.at[xl * 2 + z], rd.at[j], left)

    def back_third(j):
        got(f"bc{j}", rc.at[j])
        got(f"bd{j}", rd.at[j])
        total = p1[(d, zp)[j]].astype(F32) + rc[j].astype(F32) + rd[j].astype(F32)
        scatter_sent(6 + j, s7.at[j], y7.at[j])
        scatter_out(12 + j, s7.at[j], b7.at[j], dot(spread_ref[...], total.astype(BF)))

    def back_across(b):
        xi = row_x[b]
        got(f"bq{b}", q1.at[b])
        total = p2[xi * 2 + zlo].astype(F32) + q1[b].astype(F32)
        scatter_sent(8 + b, s6.at[b], y6.at[b])
        scatter_out(14 + b, s6.at[b], b6.at[b], dot(spread_ref[...], total.astype(BF)))

    def rows_back(b, at):
        if b < 2:
            return dot(take(at), scatter_in(12 + b, s7.at[b], b7.at[b]))
        return dot(take(at), scatter_in(12 + b, s6.at[b - 2], b6.at[b - 2]))

    def back_far():
        w2[0] = rows_back(5, dxf).astype(BF)
        go("bs0", w2.at[0, tlo], qs0, right)
        go("bs1", w2.at[0, thi], qs1, left)

    def back_right():
        w2[1] = rows_back(4, dxr).astype(BF)
        got("bs0", qs0)
        add(w2.at[1, tlo], qs0)
        go("bt0", w2.at[1], qt0, right)

    def back_left():
        w2[2] = rows_back(3, dxl).astype(BF)
        got("bs1", qs1)
        add(w2.at[2, thi], qs1)
        go("bt1", w2.at[2], qt1, left)

    def back_own():
        mine = rows_back(2, d)
        got("bt0", qt0)
        got("bt1", qt1)
        out_ref[:, c1:] = (gate * (mine + qt0[...].astype(F32) + qt1[...].astype(F32))).astype(BF)

    def back_z():
        w1[...] = rows_back(1, zp).astype(BF)
        go("bz", w1, rz, pair)

    def back_z_own():
        mine = rows_back(0, d)
        got("bz", rz)
        out_ref[:, :c1] = (gate * (mine + rz[...].astype(F32))).astype(BF)

    X = Array(0, "x", u1, u2, x7, x6, gx1, gx2)
    C = Array(1, "c", v1, v2, y7, y6, gc1, gc2)

    pl.semaphore_wait(bar, NG - 1 + 4)
    go("iz", slots.at[d], slots.at[d], pair)
    go("ir", slots.at[d], slots.at[d], right)
    go("il", slots.at[d], slots.at[d], left)
    go("if", slots.at[d], slots.at[d], far)
    X.raw_x()
    X.own1()
    X.raw_z()
    X.own2()
    C.raw_x()
    X.pass_right()
    got("iz", slots.at[zp])
    X.pair1()
    C.raw_z()
    X.pass_left()
    X.land1(0)
    got("ir", slots.at[dxl])
    X.near2(1)
    C.pass_right()
    got("il", slots.at[dxr])
    X.near2(2)
    C.pass_left()
    X.land2(0)
    got("if", slots.at[dxf])
    X.far2()
    X.land1(1)
    C.pair1()
    X.ring_left(0)
    X.land2(1)
    X.ring_right(0)
    load_in.wait()
    load_out.wait()
    X.whole(0)
    forward(x)
    X.land2(2)
    X.ring_left(1)
    X.land2(3)
    C.own1()
    X.ring_right(1)
    C.land1(1)
    C.near2(2)
    X.whole(1)
    forward(xl)
    back_pair(1)
    C.own2()
    X.whole(2)
    forward(xr)
    C.land1(0)
    C.near2(1)
    C.land2(2)
    X.whole(3)
    forward(xf)
    back_first()
    C.far2()
    C.land2(0)
    back_pair(2)
    back_across(1)
    back_pair(3)
    back_second(1)
    C.ring_left(0)
    back_second(0)
    C.land2(1)
    C.whole(0)
    backward(x)
    C.ring_left(1)
    C.ring_right(1)
    back_across(2)
    C.land2(3)
    C.whole(2)
    backward(xr)
    back_third(1)
    back_pair(0)
    back_across(3)
    C.ring_right(0)
    C.whole(1)
    backward(xl)
    back_far()
    back_z()
    back_third(0)
    C.whole(3)
    backward(xf)
    grads_out(0, 0)
    grads_out(1, 0)
    back_left()
    back_right()
    grads_in(0, 0)
    back_across(0)
    grads_out(0, 1)
    grads_in(1, 1)
    grads_in(0, 1)
    grads_in(1, 0)
    grads_out(1, 1)
    back_z_own()
    back_own()

    for b in range(6):
        scatter_sent(12 + b, s7.at[b] if b < 2 else s6.at[b - 2], b7.at[b] if b < 2 else b6.at[b - 2])
    for cp in sent:
        cp.wait_send()


def shards(tokens, cotangent, gate_prob, expert_of, w_in, w_out):
    n_tok, width = tokens.shape
    ff = w_in.shape[-1]
    c1 = width * 9 // 16
    c2 = width - c1
    o = np.arange(ROWS)
    source = (o % HALF) // CAP * SLOT + o // HALF * CAP + o % CAP
    pack = (np.arange(NG * SLOT)[None, :] == source[:, None]).astype(np.float32)
    vm = pl.BlockSpec(memory_space=pltpu.VMEM)
    hbm = pl.BlockSpec(memory_space=pl.ANY)

    def buf(*shape):
        return pltpu.VMEM(shape, BF)

    sevens = [buf(2, NG, SLOT, c1), buf(NX, NG, SLOT, c2)]
    raws = [buf(2, n_tok, c1), buf(NX, n_tok, c2)]
    gathered = [buf(ND, ROWS, c1), buf(ND, ROWS, c2)]
    return pl.pallas_call(
        functools.partial(kernel, c1, c2),
        out_shape=(
            pltpu.VMEM(tokens.shape, BF),
            pltpu.VMEM(w_in.shape, BF),
            pltpu.VMEM(w_out.shape, BF),
        ),
        in_specs=[vm] * 6 + [hbm] * 2,
        out_specs=(vm, vm, vm),
        scratch_shapes=[
            pltpu.VMEM((ND, 8, n_tok), jnp.int32),
            *raws, *raws,
            *sevens, *sevens, *sevens, *sevens,
            *gathered, *gathered,
            buf(ND, ROWS, ff), buf(ND, ROWS, ff),
            *gathered,
            buf(2, HALF, c1), buf(2, HALF, c1), buf(2, ROWS, c1), buf(2, ROWS, c1), buf(n_tok, c1),
            buf(NX, ROWS, c2), buf(n_tok // 2, c2), buf(n_tok // 2, c2), buf(n_tok, c2), buf(n_tok, c2),
            buf(n_tok, c1), buf(3, n_tok, c2),
            pltpu.SemaphoreType.DMA((2,)),
            pltpu.SemaphoreType.DMA((18,)), pltpu.SemaphoreType.DMA((18,)),
            pltpu.SemaphoreType.DMA((len(NAMES),)), pltpu.SemaphoreType.DMA((len(NAMES),)),
        ],
        compiler_params=pltpu.CompilerParams(collective_id=0, has_side_effects=True, vmem_limit_bytes=50 << 20),
        cost_estimate=pl.CostEstimate(
            flops=10 * ND * ROWS * width * ff, bytes_accessed=8 * w_in.size, transcendentals=ND * ROWS * ff
        ),
    )(
        tokens, cotangent, gate_prob.reshape(1, n_tok), expert_of.reshape(1, n_tok),
        jnp.asarray(pack, BF), jnp.asarray(pack.T, BF), w_in, w_out,
    )


def solution(mesh):
    return jax.shard_map(
        shards,
        mesh=mesh,
        in_specs=(
            P(("expert", "dp"), None),
            P(("expert", "dp"), None),
            P(("expert", "dp")),
            P(("expert", "dp"), None),
            P("expert", None, "dp"),
            P("expert", "dp", None),
        ),
        out_specs=(P(("expert", "dp"), None), P("expert", None, "dp"), P("expert", "dp", None)),
        check_vma=False,
    )
```

```python
import functools

import jax
import jax.numpy as jnp
import numpy as np
from jax import lax
from jax.experimental import pallas as pl
from jax.experimental.pallas import tpu as pltpu
from jax.sharding import PartitionSpec as P

ROOT = 0.7978845608028654
CUBIC = 0.044715
BF = jnp.bfloat16
F32 = jnp.float32
MESH = pl.DeviceIdType.MESH
CAP = 6
LOCAL = 2
SLOT = 16
NG = 16
NX = 4
ND = 8
HALF = NG * CAP
ROWS = LOCAL * HALF

ARRAY = ("rz", "rr", "rl", "hr", "hl", "xp1", "xm1", "xp1z", "xm1z", "fp1", "fm1", "fp1z", "fm1z", "z20", "z2m", "z2p", "z22")
BACK = ("a0", "a1", "b0", "b1", "c0", "c1", "d0", "d1", "q0", "q1", "q2", "q3", "s0", "s1", "t0", "t1", "z")
NAMES = (
    *("x" + n for n in ARRAY), *("c" + n for n in ARRAY), *("b" + n for n in BACK), "iz", "ir", "il", "if"
)


def gelu_pair(p):
    s = jnp.tanh(ROOT * (p + CUBIC * p * p * p))
    value = 0.5 * p * (1.0 + s)
    slope = 0.5 * (1.0 + s) + 0.5 * p * (1.0 - s * s) * ROOT * (1.0 + 3.0 * CUBIC * p * p)
    return value, slope


def dot(a, b):
    return jnp.dot(a, b, preferred_element_type=F32)


def dot_nt(a, b):
    return lax.dot_general(a, b, (((1,), (1,)), ((), ())), preferred_element_type=F32)


def dot_tn(a, b):
    return lax.dot_general(a, b, (((0,), (0,)), ((), ())), preferred_element_type=F32)


def kernel(
    c1, c2,
    tok_ref, cot_ref, gate_ref, erow_ref, pack_ref, spread_ref, win_hbm, wout_hbm,
    out_ref, win, gout,
    wout, slots, u1, u2, v1, v2, s7, s6, x7, x6, y7, y6, b7, b6,
    gx1, gx2, gc1, gc2, hid, bh, p1, p2,
    ra, rb, rc, rd, rz, q1, qs0, qs1, qt0, qt1, w1, w2,
    wsem, a_send, a_recv, n_send, n_recv,
):
    e = lax.axis_index("expert")
    d = lax.axis_index("dp")
    zhi = e // 8
    x = d // 2
    zlo = d % 2
    zot = 1 - zlo
    xr = (x + 1) % NX
    xl = (x + 3) % NX
    xf = (x + 2) % NX
    zp = x * 2 + zot
    dxr = xr * 2 + zlo
    dxl = xl * 2 + zlo
    dxf = xf * 2 + zlo
    right, left, pair, far = (e, dxr), (e, dxl), (e, zp), (e, dxf)
    n_tok, width = tok_ref.shape
    n_exp = NG * LOCAL
    n_slot = NG * SLOT

    def group_dev(g):
        cross = (zhi + g // 8) % 2
        return (g, x * 2 + (zlo + cross) % 2)

    bar = pltpu.get_barrier_semaphore()

    def greet(k, carry):
        pl.semaphore_signal(bar, inc=1, device_id=group_dev((e + k) % NG), device_id_type=MESH)
        return carry

    for dev in (right, left, pair, far):
        pl.semaphore_signal(bar, inc=1, device_id=dev, device_id_type=MESH)
    lax.fori_loop(1, NG, greet, 0)

    load_in = pltpu.make_async_copy(win_hbm, win, wsem.at[0])
    load_out = pltpu.make_async_copy(wout_hbm, wout, wsem.at[1])
    load_in.start()
    load_out.start()

    erow = erow_ref[...]
    one_row = (lax.broadcasted_iota(jnp.int32, (n_exp, n_tok), 0) == erow).astype(F32)
    before = (
        lax.broadcasted_iota(jnp.int32, (n_tok, n_tok), 0)
        < lax.broadcasted_iota(jnp.int32, (n_tok, n_tok), 1)
    ).astype(F32)
    rank = jnp.sum(dot(one_row.astype(BF), before.astype(BF)) * one_row, axis=0, keepdims=True)
    slot_row = (erow >> 1) * SLOT + (erow & 1) * CAP + rank.astype(jnp.int32)
    slots[pl.ds(d, 1)] = jnp.broadcast_to(slot_row, (8, n_tok)).reshape(1, 8, n_tok)
    eye = lax.broadcasted_iota(jnp.int32, (n_tok, n_tok), 0) == lax.broadcasted_iota(jnp.int32, (n_tok, n_tok), 1)

    def column(row):
        return jnp.sum(jnp.where(eye, row, jnp.zeros_like(row)), axis=1, keepdims=True)

    def put(b):
        row = slots[b][:1]
        return (lax.broadcasted_iota(jnp.int32, (n_slot, n_tok), 0) == row).astype(F32).astype(BF)

    def take(b):
        col = column(slots[b][:1])
        return (lax.broadcasted_iota(jnp.int32, (n_tok, n_slot), 1) == col).astype(F32).astype(BF)

    gate = column(gate_ref[...])
    u1[pl.ds(zlo, 1)] = tok_ref[:, :c1].reshape(1, n_tok, c1)
    u2[pl.ds(x, 1)] = tok_ref[:, c1:].reshape(1, n_tok, c2)
    v1[pl.ds(zlo, 1)] = (gate * cot_ref[:, :c1].astype(F32)).astype(BF).reshape(1, n_tok, c1)
    v2[pl.ds(x, 1)] = (gate * cot_ref[:, c1:].astype(F32)).astype(BF).reshape(1, n_tok, c2)

    sent = []

    def go(name, src, dst, dev):
        i = NAMES.index(name)
        cp = pltpu.make_async_remote_copy(
            src_ref=src, dst_ref=dst, send_sem=n_send.at[i], recv_sem=n_recv.at[i], device_id=dev, device_id_type=MESH
        )
        cp.start()
        sent.append(cp)

    def got(name, dst):
        i = NAMES.index(name)
        pltpu.make_async_remote_copy(
            src_ref=dst, dst_ref=dst, send_sem=n_send.at[i], recv_sem=n_recv.at[i], device_id=pair, device_id_type=MESH
        ).wait_recv()

    def across(j, src, dst):
        return pltpu.make_async_remote_copy(
            src_ref=src, dst_ref=dst, send_sem=a_send.at[j], recv_sem=a_recv.at[j], device_id=pair, device_id_type=MESH
        )

    def scatter_out(j, src, dst, value):
        src[...] = value.astype(BF).reshape(src.shape)
        dst[pl.ds(e, 1)] = src[pl.ds(e, 1)]

        def one(k, carry):
            g = (e + k) % NG
            pltpu.make_async_remote_copy(
                src_ref=src.at[g], dst_ref=dst.at[e], send_sem=a_send.at[j], recv_sem=a_recv.at[j],
                device_id=group_dev(g), device_id_type=MESH,
            ).start()
            return carry

        lax.fori_loop(1, NG, one, 0)

    others = pl.ds(0, NG - 1)

    def scatter_in(j, src, dst):
        across(j, src.at[others], dst.at[others]).wait_recv()
        return dst[...].reshape(n_slot, dst.shape[-1])

    def scatter_sent(j, src, dst):
        across(j, src.at[others], dst.at[others]).wait_send()

    lo, hi = pl.ds(0, HALF), pl.ds(HALF, HALF)
    tlo, thi = pl.ds(0, n_tok // 2), pl.ds(n_tok // 2, n_tok // 2)
    row_x = (x, xl, xr, xf)

    class Array:
        def __init__(self, i, tag, raw1, raw2, a7, a6, g1, g2):
            self.i, self.tag = i, tag
            self.raw1, self.raw2, self.a7, self.a6, self.g1, self.g2 = raw1, raw2, a7, a6, g1, g2

        def go(self, name, ref, dev):
            go(self.tag + name, ref, ref, dev)

        def got(self, name, ref):
            got(self.tag + name, ref)

        def raw_x(self):
            self.go("rr", self.raw2.at[x], right)
            self.go("rl", self.raw2.at[x], left)

        def raw_z(self):
            self.go("rz", self.raw1.at[zlo], pair)

        def free(self, b):
            if self.i > 0:
                scatter_sent(6 * self.i - 6 + b, s7.at[b] if b < 2 else s6.at[b - 2], b7.at[b] if b < 2 else b6.at[b - 2])

        def own1(self):
            self.free(0)
            scatter_out(6 * self.i, s7.at[0], self.a7.at[0], dot(put(d), self.raw1[zlo]))

        def own2(self):
            self.free(2)
            scatter_out(6 * self.i + 2, s6.at[0], self.a6.at[0], dot(put(d), self.raw2[x]))

        def pair1(self):
            self.got("rz", self.raw1.at[zot])
            self.free(1)
            scatter_out(6 * self.i + 1, s7.at[1], self.a7.at[1], dot(put(zp), self.raw1[zot]))

        def pass_right(self):
            self.got("rr", self.raw2.at[xl])
            self.go("hr", self.raw2.at[xl, tlo], right)

        def pass_left(self):
            self.got("rl", self.raw2.at[xr])
            self.go("hl", self.raw2.at[xr, thi], left)

        def near2(self, b):
            xi = row_x[b]
            self.free(2 + b)
            scatter_out(6 * self.i + 2 + b, s6.at[b], self.a6.at[b], dot(put(xi * 2 + zlo), self.raw2[xi]))

        def far2(self):
            self.got("hr", self.raw2.at[xf, tlo])
            self.got("hl", self.raw2.at[xf, thi])
            self.free(5)
            scatter_out(6 * self.i + 5, s6.at[3], self.a6.at[3], dot(put(dxf), self.raw2[xf]))

        def land1(self, b):
            rows = scatter_in(6 * self.i + b, s7.at[b], self.a7.at[b])
            at = (d, zp)[b]
            self.g1[pl.ds(at, 1)] = dot(pack_ref[...], rows).astype(BF).reshape(1, ROWS, c1)
            self.go(("xp1", "xp1z")[b], self.g1.at[at], right)
            self.go(("xm1", "xm1z")[b], self.g1.at[at], left)

        def land2(self, b):
            rows = scatter_in(6 * self.i + 2 + b, s6.at[b], self.a6.at[b])
            at = row_x[b] * 2 + zlo
            self.g2[pl.ds(at, 1)] = dot(pack_ref[...], rows).astype(BF).reshape(1, ROWS, c2)
            self.go(("z20", "z2m", "z2p", "z22")[b], self.g2.at[at], pair)

        def ring_right(self, b):
            g1, z, t = self.g1, (zlo, zot)[b], ("", "z")[b]
            self.got("xp1" + t, g1.at[xl * 2 + z])
            self.go("fp1" + t, g1.at[xl * 2 + z, lo], right)

        def ring_left(self, b):
            g1, z, t = self.g1, (zlo, zot)[b], ("", "z")[b]
            self.got("xm1" + t, g1.at[xr * 2 + z])
            self.go("fm1" + t, g1.at[xr * 2 + z, hi], left)

        def whole(self, b):
            if b == 3:
                for z, t in ((zlo, ""), (zot, "z")):
                    self.got("fp1" + t, self.g1.at[xf * 2 + z, lo])
                    self.got("fm1" + t, self.g1.at[xf * 2 + z, hi])
            self.got(("z20", "z2m", "z2p", "z22")[b], self.g2.at[row_x[b] * 2 + zot])

    def block(ref, xi, le):
        return ref[pl.ds(2 * xi, 2), pl.ds(pl.multiple_of(le * HALF, 32), HALF), :].reshape(2 * HALF, ref.shape[-1])

    def keep(ref, xi, le, value):
        ref[pl.ds(2 * xi, 2), pl.ds(pl.multiple_of(le * HALF, 32), HALF), :] = value.reshape(2, HALF, ref.shape[-1])

    def forward(xi):
        def one(le, carry):
            pre = dot(block(gx1, xi, le), win[le, :c1, :]) + dot(block(gx2, xi, le), win[le, c1:, :])
            value, slope = gelu_pair(pre)
            h = value.astype(BF)
            keep(hid, xi, le, h)
            keep(bh, xi, le, slope.astype(BF))
            keep(p1, xi, le, dot(h, wout[le, :, :c1]).astype(BF))
            keep(p2, xi, le, dot(h, wout[le, :, c1:]).astype(BF))
            return carry

        lax.fori_loop(0, LOCAL, one, 0)

    def backward(xi):
        def one(le, carry):
            b = dot_nt(block(gc1, xi, le), wout[le, :, :c1]) + dot_nt(block(gc2, xi, le), wout[le, :, c1:])
            keep(bh, xi, le, (b * block(bh, xi, le).astype(F32)).astype(BF))
            return carry

        lax.fori_loop(0, LOCAL, one, 0)

    def early(ref, le):
        return jnp.concatenate([block(ref, xi, le) for xi in (x, xl, xr)], axis=0)

    parts = ((pl.ds(0, c1), gx1, gc1), (pl.ds(c1, c2), gx2, gc2))

    def grads_in(le, part):
        at, gx, _ = parts[part]
        win[le, at, :] = dot_tn(early(gx, le), early(bh, le)).astype(BF)

    def grads_out(le, part):
        at, _, gc = parts[part]
        gout[le, :, at] = dot_tn(early(hid, le), early(gc, le)).astype(BF)

    def last_in(le, part):
        at, gx, _ = parts[part]
        win[le, at, :] = (win[le, at, :].astype(F32) + dot_tn(block(gx, xf, le), block(bh, xf, le))).astype(BF)

    def last_out(le, part):
        at, _, gc = parts[part]
        gout[le, :, at] = (gout[le, :, at].astype(F32) + dot_tn(block(hid, xf, le), block(gc, xf, le))).astype(BF)

    def add(dst, src):
        dst[...] = (dst[...].astype(F32) + src[...].astype(F32)).astype(BF)

    zs = ((0, zlo), (1, zot))
    def back_first():
        for j, z in zs[::-1]:
            go(f"ba{j}", p1.at[xf * 2 + z, lo], ra.at[j], right)
            go(f"bb{j}", p1.at[xf * 2 + z, hi], rb.at[j], left)

    def back_pair(b):
        xi = row_x[b]
        go(f"bq{b}", p2.at[xi * 2 + zot], q1.at[b], pair)

    def back_second(j):
        z = (zlo, zot)[j]
        got(f"ba{j}", ra.at[j])
        add(p1.at[xr * 2 + z, lo], ra.at[j])
        go(f"bc{j}", p1.at[xr * 2 + z], rc.at[j], right)
        got(f"bb{j}", rb.at[j])
        add(p1.at[xl * 2 + z, hi], rb.at[j])
        go(f"bd{j}", p1.at[xl * 2 + z], rd.at[j], left)

    def back_third(j):
        got(f"bc{j}", rc.at[j])
        got(f"bd{j}", rd.at[j])
        total = p1[(d, zp)[j]].astype(F32) + rc[j].astype(F32) + rd[j].astype(F32)
        scatter_sent(6 + j, s7.at[j], y7.at[j])
        scatter_out(12 + j, s7.at[j], b7.at[j], dot(spread_ref[...], total.astype(BF)))

    def back_across(b):
        xi = row_x[b]
        got(f"bq{b}", q1.at[b])
        total = p2[xi * 2 + zlo].astype(F32) + q1[b].astype(F32)
        scatter_sent(8 + b, s6.at[b], y6.at[b])
        scatter_out(14 + b, s6.at[b], b6.at[b], dot(spread_ref[...], total.astype(BF)))

    def rows_back(b, at):
        if b < 2:
            return dot(take(at), scatter_in(12 + b, s7.at[b], b7.at[b]))
        return dot(take(at), scatter_in(12 + b, s6.at[b - 2], b6.at[b - 2]))

    def back_far():
        w2[0] = rows_back(5, dxf).astype(BF)
        go("bs0", w2.at[0, tlo], qs0, right)
        go("bs1", w2.at[0, thi], qs1, left)

    def back_right():
        w2[1] = rows_back(4, dxr).astype(BF)
        got("bs0", qs0)
        add(w2.at[1, tlo], qs0)
        go("bt0", w2.at[1], qt0, right)

    def back_left():
        w2[2] = rows_back(3, dxl).astype(BF)
        got("bs1", qs1)
        add(w2.at[2, thi], qs1)
        go("bt1", w2.at[2], qt1, left)

    def back_own():
        mine = rows_back(2, d)
        got("bt0", qt0)
        got("bt1", qt1)
        out_ref[:, c1:] = (gate * (mine + qt0[...].astype(F32) + qt1[...].astype(F32))).astype(BF)

    def back_z():
        w1[...] = rows_back(1, zp).astype(BF)
        go("bz", w1, rz, pair)

    def back_z_own():
        mine = rows_back(0, d)
        got("bz", rz)
        out_ref[:, :c1] = (gate * (mine + rz[...].astype(F32))).astype(BF)

    X = Array(0, "x", u1, u2, x7, x6, gx1, gx2)
    C = Array(1, "c", v1, v2, y7, y6, gc1, gc2)

    pl.semaphore_wait(bar, NG - 1 + 4)
    go("iz", slots.at[d], slots.at[d], pair)
    go("ir", slots.at[d], slots.at[d], right)
    go("il", slots.at[d], slots.at[d], left)
    go("if", slots.at[d], slots.at[d], far)
    X.raw_x()
    X.own1()
    C.raw_x()
    X.raw_z()
    X.own2()
    X.pass_right()
    C.raw_z()
    X.land1(0)
    X.pass_left()
    got("il", slots.at[dxr])
    X.near2(2)
    got("iz", slots.at[zp])
    X.pair1()
    X.land2(0)
    got("ir", slots.at[dxl])
    X.near2(1)
    X.land2(2)
    X.ring_left(0)
    C.pass_right()
    X.land1(1)
    got("if", slots.at[dxf])
    X.far2()
    X.ring_right(0)
    X.land2(1)
    C.own1()
    C.near2(1)
    C.pass_left()
    C.own2()
    X.land2(3)
    C.near2(2)
    X.ring_left(1)
    X.ring_right(1)
    load_in.wait()
    load_out.wait()
    X.whole(1)
    forward(xl)
    back_pair(1)
    C.land1(0)
    X.whole(3)
    forward(xf)
    back_pair(3)
    back_first()
    C.pair1()
    C.land2(0)
    X.whole(2)
    forward(xr)
    C.land1(1)
    back_second(1)
    C.far2()
    C.land2(2)
    X.whole(0)
    forward(x)
    C.land2(1)
    back_pair(2)
    back_second(0)
    C.ring_right(0)
    back_across(3)
    back_across(1)
    C.ring_left(0)
    C.whole(0)
    backward(x)
    back_far()
    C.ring_left(1)
    back_pair(0)
    C.whole(2)
    backward(xr)
    C.ring_right(1)
    C.whole(1)
    backward(xl)
    back_third(1)
    grads_in(1, 1)
    C.land2(3)
    grads_in(0, 1)
    grads_out(1, 1)
    back_across(2)
    grads_out(1, 0)
    grads_in(0, 0)
    back_third(0)
    grads_out(0, 1)
    grads_out(0, 0)
    back_z()
    back_right()
    back_across(0)
    grads_in(1, 0)
    back_left()
    C.whole(3)
    backward(xf)
    last_in(0, 1)
    last_in(1, 1)
    last_out(1, 0)
    last_out(0, 1)
    last_in(0, 0)
    last_out(0, 0)
    last_in(1, 0)
    last_out(1, 1)
    back_z_own()
    back_own()

    for b in range(6):
        scatter_sent(12 + b, s7.at[b] if b < 2 else s6.at[b - 2], b7.at[b] if b < 2 else b6.at[b - 2])
    for cp in sent:
        cp.wait_send()


def shards(tokens, cotangent, gate_prob, expert_of, w_in, w_out):
    n_tok, width = tokens.shape
    ff = w_in.shape[-1]
    c1 = width * 9 // 16
    c2 = width - c1
    o = np.arange(ROWS)
    source = (o % HALF) // CAP * SLOT + o // HALF * CAP + o % CAP
    pack = (np.arange(NG * SLOT)[None, :] == source[:, None]).astype(np.float32)
    vm = pl.BlockSpec(memory_space=pltpu.VMEM)
    hbm = pl.BlockSpec(memory_space=pl.ANY)

    def buf(*shape):
        return pltpu.VMEM(shape, BF)

    sevens = [buf(2, NG, SLOT, c1), buf(NX, NG, SLOT, c2)]
    raws = [buf(2, n_tok, c1), buf(NX, n_tok, c2)]
    gathered = [buf(ND, ROWS, c1), buf(ND, ROWS, c2)]
    return pl.pallas_call(
        functools.partial(kernel, c1, c2),
        out_shape=(
            pltpu.VMEM(tokens.shape, BF),
            pltpu.VMEM(w_in.shape, BF),
            pltpu.VMEM(w_out.shape, BF),
        ),
        in_specs=[vm] * 6 + [hbm] * 2,
        out_specs=(vm, vm, vm),
        scratch_shapes=[
            buf(*w_out.shape),
            pltpu.VMEM((ND, 8, n_tok), jnp.int32),
            *raws, *raws,
            *sevens, *sevens, *sevens, *sevens,
            *gathered, *gathered,
            buf(ND, ROWS, ff), buf(ND, ROWS, ff),
            *gathered,
            buf(2, HALF, c1), buf(2, HALF, c1), buf(2, ROWS, c1), buf(2, ROWS, c1), buf(n_tok, c1),
            buf(NX, ROWS, c2), buf(n_tok // 2, c2), buf(n_tok // 2, c2), buf(n_tok, c2), buf(n_tok, c2),
            buf(n_tok, c1), buf(3, n_tok, c2),
            pltpu.SemaphoreType.DMA((2,)),
            pltpu.SemaphoreType.DMA((18,)), pltpu.SemaphoreType.DMA((18,)),
            pltpu.SemaphoreType.DMA((len(NAMES),)), pltpu.SemaphoreType.DMA((len(NAMES),)),
        ],
        compiler_params=pltpu.CompilerParams(collective_id=0, has_side_effects=True, vmem_limit_bytes=53 << 20),
        cost_estimate=pl.CostEstimate(
            flops=10 * ND * ROWS * width * ff, bytes_accessed=8 * w_in.size, transcendentals=ND * ROWS * ff
        ),
    )(
        tokens, cotangent, gate_prob.reshape(1, n_tok), expert_of.reshape(1, n_tok),
        jnp.asarray(pack, BF), jnp.asarray(pack.T, BF), w_in, w_out,
    )


def solution(mesh):
    return jax.shard_map(
        shards,
        mesh=mesh,
        in_specs=(
            P(("expert", "dp"), None),
            P(("expert", "dp"), None),
            P(("expert", "dp")),
            P(("expert", "dp"), None),
            P("expert", None, "dp"),
            P("expert", "dp", None),
        ),
        out_specs=(P(("expert", "dp"), None), P("expert", None, "dp"), P("expert", "dp", None)),
        check_vma=False,
    )
```

```python
import functools

import jax
import jax.numpy as jnp
import numpy as np
from jax import lax
from jax.experimental import pallas as pl
from jax.experimental.pallas import tpu as pltpu
from jax.sharding import PartitionSpec as P

ROOT = 0.7978845608028654
CUBIC = 0.044715
BF = jnp.bfloat16
F32 = jnp.float32
MESH = pl.DeviceIdType.MESH
CAP = 6
LOCAL = 2
SLOT = 16
NG = 16
NX = 4
ND = 8
HALF = NG * CAP
ROWS = LOCAL * HALF

ARRAY = ("rz", "rr", "rl", "hr", "hl", "xp1", "xm1", "xp1z", "xm1z", "fp1", "fm1", "fp1z", "fm1z", "z20", "z2m", "z2p", "z22")
BACK = ("a0", "a1", "b0", "b1", "c0", "c1", "d0", "d1", "q0", "q1", "q2", "q3", "s0", "s1", "t0", "t1", "z")
NAMES = (
    *("x" + n for n in ARRAY), *("c" + n for n in ARRAY), *("b" + n for n in BACK), "iz", "ir", "il", "if"
)


def gelu_pair(p):
    s = jnp.tanh(ROOT * (p + CUBIC * p * p * p))
    value = 0.5 * p * (1.0 + s)
    slope = 0.5 * (1.0 + s) + 0.5 * p * (1.0 - s * s) * ROOT * (1.0 + 3.0 * CUBIC * p * p)
    return value, slope


def dot(a, b):
    return jnp.dot(a, b, preferred_element_type=F32)


def dot_nt(a, b):
    return lax.dot_general(a, b, (((1,), (1,)), ((), ())), preferred_element_type=F32)


def dot_tn(a, b):
    return lax.dot_general(a, b, (((0,), (0,)), ((), ())), preferred_element_type=F32)


def kernel(
    c1, c2,
    tok_ref, cot_ref, gate_ref, erow_ref, pack_ref, spread_ref, win_hbm, wout_hbm,
    out_ref, win, gout,
    wout, slots, u1, u2, v1, v2, s7, s6, x7, x6, y7, y6, b7, b6,
    gx1, gx2, gc1, gc2, hid, bh, p1, p2,
    ra, rb, rc, rd, rz, q1, qs0, qs1, qt0, qt1, w1, w2,
    wsem, a_send, a_recv, n_send, n_recv,
):
    e = lax.axis_index("expert")
    d = lax.axis_index("dp")
    zhi = e // 8
    x = d // 2
    zlo = d % 2
    zot = 1 - zlo
    xr = (x + 1) % NX
    xl = (x + 3) % NX
    xf = (x + 2) % NX
    zp = x * 2 + zot
    dxr = xr * 2 + zlo
    dxl = xl * 2 + zlo
    dxf = xf * 2 + zlo
    right, left, pair, far = (e, dxr), (e, dxl), (e, zp), (e, dxf)
    n_tok, width = tok_ref.shape
    n_exp = NG * LOCAL
    n_slot = NG * SLOT

    def group_dev(g):
        cross = (zhi + g // 8) % 2
        return (g, x * 2 + (zlo + cross) % 2)

    bar = pltpu.get_barrier_semaphore()

    def greet(k, carry):
        pl.semaphore_signal(bar, inc=1, device_id=group_dev((e + k) % NG), device_id_type=MESH)
        return carry

    for dev in (right, left, pair, far):
        pl.semaphore_signal(bar, inc=1, device_id=dev, device_id_type=MESH)
    lax.fori_loop(1, NG, greet, 0)

    load_in = pltpu.make_async_copy(win_hbm, win, wsem.at[0])
    load_out = pltpu.make_async_copy(wout_hbm, wout, wsem.at[1])
    load_in.start()
    load_out.start()

    erow = erow_ref[...]
    one_row = (lax.broadcasted_iota(jnp.int32, (n_exp, n_tok), 0) == erow).astype(F32)
    before = (
        lax.broadcasted_iota(jnp.int32, (n_tok, n_tok), 0)
        < lax.broadcasted_iota(jnp.int32, (n_tok, n_tok), 1)
    ).astype(F32)
    rank = jnp.sum(dot(one_row.astype(BF), before.astype(BF)) * one_row, axis=0, keepdims=True)
    slot_row = (erow >> 1) * SLOT + (erow & 1) * CAP + rank.astype(jnp.int32)
    slots[pl.ds(d, 1)] = jnp.broadcast_to(slot_row, (8, n_tok)).reshape(1, 8, n_tok)
    eye = lax.broadcasted_iota(jnp.int32, (n_tok, n_tok), 0) == lax.broadcasted_iota(jnp.int32, (n_tok, n_tok), 1)

    def column(row):
        return jnp.sum(jnp.where(eye, row, jnp.zeros_like(row)), axis=1, keepdims=True)

    def put(b):
        row = slots[b][:1]
        return (lax.broadcasted_iota(jnp.int32, (n_slot, n_tok), 0) == row).astype(F32).astype(BF)

    def take(b):
        col = column(slots[b][:1])
        return (lax.broadcasted_iota(jnp.int32, (n_tok, n_slot), 1) == col).astype(F32).astype(BF)

    gate = column(gate_ref[...])
    u1[pl.ds(zlo, 1)] = tok_ref[:, :c1].reshape(1, n_tok, c1)
    u2[pl.ds(x, 1)] = tok_ref[:, c1:].reshape(1, n_tok, c2)
    v1[pl.ds(zlo, 1)] = (gate * cot_ref[:, :c1].astype(F32)).astype(BF).reshape(1, n_tok, c1)
    v2[pl.ds(x, 1)] = (gate * cot_ref[:, c1:].astype(F32)).astype(BF).reshape(1, n_tok, c2)

    sent = []

    def go(name, src, dst, dev):
        i = NAMES.index(name)
        cp = pltpu.make_async_remote_copy(
            src_ref=src, dst_ref=dst, send_sem=n_send.at[i], recv_sem=n_recv.at[i], device_id=dev, device_id_type=MESH
        )
        cp.start()
        sent.append(cp)

    def got(name, dst):
        i = NAMES.index(name)
        pltpu.make_async_remote_copy(
            src_ref=dst, dst_ref=dst, send_sem=n_send.at[i], recv_sem=n_recv.at[i], device_id=pair, device_id_type=MESH
        ).wait_recv()

    def across(j, src, dst):
        return pltpu.make_async_remote_copy(
            src_ref=src, dst_ref=dst, send_sem=a_send.at[j], recv_sem=a_recv.at[j], device_id=pair, device_id_type=MESH
        )

    def scatter_out(j, src, dst, value):
        src[...] = value.astype(BF).reshape(src.shape)
        dst[pl.ds(e, 1)] = src[pl.ds(e, 1)]

        def one(k, carry):
            g = (e + k) % NG
            pltpu.make_async_remote_copy(
                src_ref=src.at[g], dst_ref=dst.at[e], send_sem=a_send.at[j], recv_sem=a_recv.at[j],
                device_id=group_dev(g), device_id_type=MESH,
            ).start()
            return carry

        lax.fori_loop(1, NG, one, 0)

    others = pl.ds(0, NG - 1)

    def scatter_in(j, src, dst):
        across(j, src.at[others], dst.at[others]).wait_recv()
        return dst[...].reshape(n_slot, dst.shape[-1])

    def scatter_sent(j, src, dst):
        across(j, src.at[others], dst.at[others]).wait_send()

    lo, hi = pl.ds(0, HALF), pl.ds(HALF, HALF)
    tlo, thi = pl.ds(0, n_tok // 2), pl.ds(n_tok // 2, n_tok // 2)
    row_x = (x, xl, xr, xf)

    class Array:
        def __init__(self, i, tag, raw1, raw2, a7, a6, g1, g2):
            self.i, self.tag = i, tag
            self.raw1, self.raw2, self.a7, self.a6, self.g1, self.g2 = raw1, raw2, a7, a6, g1, g2

        def go(self, name, ref, dev):
            go(self.tag + name, ref, ref, dev)

        def got(self, name, ref):
            got(self.tag + name, ref)

        def raw_x(self):
            self.go("rr", self.raw2.at[x], right)
            self.go("rl", self.raw2.at[x], left)

        def raw_z(self):
            self.go("rz", self.raw1.at[zlo], pair)

        def free(self, b):
            if self.i > 0:
                scatter_sent(6 * self.i - 6 + b, s7.at[b] if b < 2 else s6.at[b - 2], b7.at[b] if b < 2 else b6.at[b - 2])

        def own1(self):
            self.free(0)
            scatter_out(6 * self.i, s7.at[0], self.a7.at[0], dot(put(d), self.raw1[zlo]))

        def own2(self):
            self.free(2)
            scatter_out(6 * self.i + 2, s6.at[0], self.a6.at[0], dot(put(d), self.raw2[x]))

        def pair1(self):
            self.got("rz", self.raw1.at[zot])
            self.free(1)
            scatter_out(6 * self.i + 1, s7.at[1], self.a7.at[1], dot(put(zp), self.raw1[zot]))

        def pass_right(self):
            self.got("rr", self.raw2.at[xl])
            self.go("hr", self.raw2.at[xl, tlo], right)

        def pass_left(self):
            self.got("rl", self.raw2.at[xr])
            self.go("hl", self.raw2.at[xr, thi], left)

        def near2(self, b):
            xi = row_x[b]
            self.free(2 + b)
            scatter_out(6 * self.i + 2 + b, s6.at[b], self.a6.at[b], dot(put(xi * 2 + zlo), self.raw2[xi]))

        def far2(self):
            self.got("hr", self.raw2.at[xf, tlo])
            self.got("hl", self.raw2.at[xf, thi])
            self.free(5)
            scatter_out(6 * self.i + 5, s6.at[3], self.a6.at[3], dot(put(dxf), self.raw2[xf]))

        def land1(self, b):
            rows = scatter_in(6 * self.i + b, s7.at[b], self.a7.at[b])
            at = (d, zp)[b]
            self.g1[pl.ds(at, 1)] = dot(pack_ref[...], rows).astype(BF).reshape(1, ROWS, c1)
            self.go(("xp1", "xp1z")[b], self.g1.at[at], right)
            self.go(("xm1", "xm1z")[b], self.g1.at[at], left)

        def land2(self, b):
            rows = scatter_in(6 * self.i + 2 + b, s6.at[b], self.a6.at[b])
            at = row_x[b] * 2 + zlo
            self.g2[pl.ds(at, 1)] = dot(pack_ref[...], rows).astype(BF).reshape(1, ROWS, c2)
            self.go(("z20", "z2m", "z2p", "z22")[b], self.g2.at[at], pair)

        def ring_right(self, b):
            g1, z, t = self.g1, (zlo, zot)[b], ("", "z")[b]
            self.got("xp1" + t, g1.at[xl * 2 + z])
            self.go("fp1" + t, g1.at[xl * 2 + z, lo], right)

        def ring_left(self, b):
            g1, z, t = self.g1, (zlo, zot)[b], ("", "z")[b]
            self.got("xm1" + t, g1.at[xr * 2 + z])
            self.go("fm1" + t, g1.at[xr * 2 + z, hi], left)

        def whole(self, b):
            if b == 3:
                for z, t in ((zlo, ""), (zot, "z")):
                    self.got("fp1" + t, self.g1.at[xf * 2 + z, lo])
                    self.got("fm1" + t, self.g1.at[xf * 2 + z, hi])
            self.got(("z20", "z2m", "z2p", "z22")[b], self.g2.at[row_x[b] * 2 + zot])

    def block(ref, xi, le):
        return ref[pl.ds(2 * xi, 2), pl.ds(pl.multiple_of(le * HALF, 32), HALF), :].reshape(2 * HALF, ref.shape[-1])

    def keep(ref, xi, le, value):
        ref[pl.ds(2 * xi, 2), pl.ds(pl.multiple_of(le * HALF, 32), HALF), :] = value.reshape(2, HALF, ref.shape[-1])

    def forward(xi):
        def one(le, carry):
            pre = dot(block(gx1, xi, le), win[le, :c1, :]) + dot(block(gx2, xi, le), win[le, c1:, :])
            value, slope = gelu_pair(pre)
            h = value.astype(BF)
            keep(hid, xi, le, h)
            keep(bh, xi, le, slope.astype(BF))
            keep(p1, xi, le, dot(h, wout[le, :, :c1]).astype(BF))
            keep(p2, xi, le, dot(h, wout[le, :, c1:]).astype(BF))
            return carry

        lax.fori_loop(0, LOCAL, one, 0)

    def backward(xi):
        def one(le, carry):
            b = dot_nt(block(gc1, xi, le), wout[le, :, :c1]) + dot_nt(block(gc2, xi, le), wout[le, :, c1:])
            keep(bh, xi, le, (b * block(bh, xi, le).astype(F32)).astype(BF))
            return carry

        lax.fori_loop(0, LOCAL, one, 0)

    def early(ref, le):
        return jnp.concatenate([block(ref, xi, le) for xi in (x, xl, xr)], axis=0)

    parts = ((pl.ds(0, c1), gx1, gc1), (pl.ds(c1, c2), gx2, gc2))

    def grads_in(le, part):
        at, gx, _ = parts[part]
        win[le, at, :] = dot_tn(early(gx, le), early(bh, le)).astype(BF)

    def grads_out(le, part):
        at, _, gc = parts[part]
        gout[le, :, at] = dot_tn(early(hid, le), early(gc, le)).astype(BF)

    def last_in(le, part):
        at, gx, _ = parts[part]
        win[le, at, :] = (win[le, at, :].astype(F32) + dot_tn(block(gx, xf, le), block(bh, xf, le))).astype(BF)

    def last_out(le, part):
        at, _, gc = parts[part]
        gout[le, :, at] = (gout[le, :, at].astype(F32) + dot_tn(block(hid, xf, le), block(gc, xf, le))).astype(BF)

    def add(dst, src):
        dst[...] = (dst[...].astype(F32) + src[...].astype(F32)).astype(BF)

    zs = ((0, zlo), (1, zot))
    def back_first():
        for j, z in zs[::-1]:
            go(f"ba{j}", p1.at[xf * 2 + z, lo], ra.at[j], right)
            go(f"bb{j}", p1.at[xf * 2 + z, hi], rb.at[j], left)

    def back_pair(b):
        xi = row_x[b]
        go(f"bq{b}", p2.at[xi * 2 + zot], q1.at[b], pair)

    def back_second(j):
        z = (zlo, zot)[j]
        got(f"ba{j}", ra.at[j])
        add(p1.at[xr * 2 + z, lo], ra.at[j])
        go(f"bc{j}", p1.at[xr * 2 + z], rc.at[j], right)
        got(f"bb{j}", rb.at[j])
        add(p1.at[xl * 2 + z, hi], rb.at[j])
        go(f"bd{j}", p1.at[xl * 2 + z], rd.at[j], left)

    def back_third(j):
        got(f"bc{j}", rc.at[j])
        got(f"bd{j}", rd.at[j])
        total = p1[(d, zp)[j]].astype(F32) + rc[j].astype(F32) + rd[j].astype(F32)
        scatter_sent(6 + j, s7.at[j], y7.at[j])
        scatter_out(12 + j, s7.at[j], b7.at[j], dot(spread_ref[...], total.astype(BF)))

    def back_across(b):
        xi = row_x[b]
        got(f"bq{b}", q1.at[b])
        total = p2[xi * 2 + zlo].astype(F32) + q1[b].astype(F32)
        scatter_sent(8 + b, s6.at[b], y6.at[b])
        scatter_out(14 + b, s6.at[b], b6.at[b], dot(spread_ref[...], total.astype(BF)))

    def rows_back(b, at):
        if b < 2:
            return dot(take(at), scatter_in(12 + b, s7.at[b], b7.at[b]))
        return dot(take(at), scatter_in(12 + b, s6.at[b - 2], b6.at[b - 2]))

    def back_far():
        w2[0] = rows_back(5, dxf).astype(BF)
        go("bs0", w2.at[0, tlo], qs0, right)
        go("bs1", w2.at[0, thi], qs1, left)

    def back_right():
        w2[1] = rows_back(4, dxr).astype(BF)
        got("bs0", qs0)
        add(w2.at[1, tlo], qs0)
        go("bt0", w2.at[1], qt0, right)

    def back_left():
        w2[2] = rows_back(3, dxl).astype(BF)
        got("bs1", qs1)
        add(w2.at[2, thi], qs1)
        go("bt1", w2.at[2], qt1, left)

    def back_own():
        mine = rows_back(2, d)
        got("bt0", qt0)
        got("bt1", qt1)
        out_ref[:, c1:] = (gate * (mine + qt0[...].astype(F32) + qt1[...].astype(F32))).astype(BF)

    def back_z():
        w1[...] = rows_back(1, zp).astype(BF)
        go("bz", w1, rz, pair)

    def back_z_own():
        mine = rows_back(0, d)
        got("bz", rz)
        out_ref[:, :c1] = (gate * (mine + rz[...].astype(F32))).astype(BF)

    X = Array(0, "x", u1, u2, x7, x6, gx1, gx2)
    C = Array(1, "c", v1, v2, y7, y6, gc1, gc2)

    pl.semaphore_wait(bar, NG - 1 + 4)
    go("iz", slots.at[d], slots.at[d], pair)
    go("ir", slots.at[d], slots.at[d], right)
    go("il", slots.at[d], slots.at[d], left)
    go("if", slots.at[d], slots.at[d], far)
    C.raw_z()
    X.raw_x()
    X.own1()
    X.own2()
    C.raw_x()
    X.raw_z()
    X.land1(0)
    X.pass_right()
    got("ir", slots.at[dxl])
    X.near2(1)
    got("iz", slots.at[zp])
    X.pair1()
    X.land2(0)
    X.pass_left()
    C.pass_left()
    X.ring_right(0)
    got("il", slots.at[dxr])
    X.near2(2)
    X.land2(1)
    X.land1(1)
    X.ring_left(0)
    got("if", slots.at[dxf])
    X.far2()
    X.land2(2)
    C.own1()
    C.own2()
    C.pass_right()
    C.pair1()
    X.land2(3)
    X.ring_right(1)
    X.ring_left(1)
    load_in.wait()
    load_out.wait()
    X.whole(1)
    forward(xl)
    back_pair(1)
    C.land1(0)
    X.whole(2)
    forward(xr)
    C.near2(2)
    C.near2(1)
    back_pair(2)
    X.whole(3)
    forward(xf)
    back_first()
    X.whole(0)
    forward(x)
    C.land2(2)
    C.land2(0)
    C.land1(1)
    C.far2()
    back_across(2)
    back_second(1)
    C.land2(1)
    C.whole(0)
    backward(x)
    back_pair(3)
    back_second(0)
    C.land2(3)
    back_across(1)
    C.ring_left(0)
    C.ring_right(0)
    C.ring_right(1)
    C.ring_left(1)
    C.whole(2)
    backward(xr)
    C.whole(1)
    backward(xl)
    back_pair(0)
    back_third(1)
    grads_out(1, 0)
    grads_out(1, 1)
    grads_in(0, 1)
    back_across(3)
    grads_out(0, 1)
    grads_in(1, 1)
    grads_in(0, 0)
    back_third(0)
    grads_out(0, 0)
    back_far()
    back_z()
    grads_in(1, 0)
    C.whole(3)
    backward(xf)
    back_right()
    back_across(0)
    back_left()
    last_out(1, 0)
    last_in(1, 1)
    last_in(0, 0)
    last_out(1, 1)
    last_in(0, 1)
    last_in(1, 0)
    last_out(0, 0)
    last_out(0, 1)
    back_z_own()
    back_own()

    for b in range(6):
        scatter_sent(12 + b, s7.at[b] if b < 2 else s6.at[b - 2], b7.at[b] if b < 2 else b6.at[b - 2])
    for cp in sent:
        cp.wait_send()


def shards(tokens, cotangent, gate_prob, expert_of, w_in, w_out):
    n_tok, width = tokens.shape
    ff = w_in.shape[-1]
    c1 = width * 9 // 16
    c2 = width - c1
    o = np.arange(ROWS)
    source = (o % HALF) // CAP * SLOT + o // HALF * CAP + o % CAP
    pack = (np.arange(NG * SLOT)[None, :] == source[:, None]).astype(np.float32)
    vm = pl.BlockSpec(memory_space=pltpu.VMEM)
    hbm = pl.BlockSpec(memory_space=pl.ANY)

    def buf(*shape):
        return pltpu.VMEM(shape, BF)

    sevens = [buf(2, NG, SLOT, c1), buf(NX, NG, SLOT, c2)]
    raws = [buf(2, n_tok, c1), buf(NX, n_tok, c2)]
    gathered = [buf(ND, ROWS, c1), buf(ND, ROWS, c2)]
    return pl.pallas_call(
        functools.partial(kernel, c1, c2),
        out_shape=(
            pltpu.VMEM(tokens.shape, BF),
            pltpu.VMEM(w_in.shape, BF),
            pltpu.VMEM(w_out.shape, BF),
        ),
        in_specs=[vm] * 6 + [hbm] * 2,
        out_specs=(vm, vm, vm),
        scratch_shapes=[
            buf(*w_out.shape),
            pltpu.VMEM((ND, 8, n_tok), jnp.int32),
            *raws, *raws,
            *sevens, *sevens, *sevens, *sevens,
            *gathered, *gathered,
            buf(ND, ROWS, ff), buf(ND, ROWS, ff),
            *gathered,
            buf(2, HALF, c1), buf(2, HALF, c1), buf(2, ROWS, c1), buf(2, ROWS, c1), buf(n_tok, c1),
            buf(NX, ROWS, c2), buf(n_tok // 2, c2), buf(n_tok // 2, c2), buf(n_tok, c2), buf(n_tok, c2),
            buf(n_tok, c1), buf(3, n_tok, c2),
            pltpu.SemaphoreType.DMA((2,)),
            pltpu.SemaphoreType.DMA((18,)), pltpu.SemaphoreType.DMA((18,)),
            pltpu.SemaphoreType.DMA((len(NAMES),)), pltpu.SemaphoreType.DMA((len(NAMES),)),
        ],
        compiler_params=pltpu.CompilerParams(collective_id=0, has_side_effects=True, vmem_limit_bytes=53 << 20),
        cost_estimate=pl.CostEstimate(
            flops=10 * ND * ROWS * width * ff, bytes_accessed=8 * w_in.size, transcendentals=ND * ROWS * ff
        ),
    )(
        tokens, cotangent, gate_prob.reshape(1, n_tok), expert_of.reshape(1, n_tok),
        jnp.asarray(pack, BF), jnp.asarray(pack.T, BF), w_in, w_out,
    )


def solution(mesh):
    return jax.shard_map(
        shards,
        mesh=mesh,
        in_specs=(
            P(("expert", "dp"), None),
            P(("expert", "dp"), None),
            P(("expert", "dp")),
            P(("expert", "dp"), None),
            P("expert", None, "dp"),
            P("expert", "dp", None),
        ),
        out_specs=(P(("expert", "dp"), None), P("expert", None, "dp"), P("expert", "dp", None)),
        check_vma=False,
    )
```
